256 devices in a mesh: plane: 32 (over x, z), depth: 8 (over y, core).
Axes of the slice: x: 4, y: 4, z: 8, core: 2. Of those that a mesh axis runs over, the one named last changes fastest.
Arguments:
- density: float32 [64, 262144], P(None, ('plane', 'depth')), may hold values from 0.01 to 1
- energy: float32 [64, 262144], P(None, ('plane', 'depth')), may hold values from 0.1 to 10
- links: int32 [27, 262144], P(None, ('plane', 'depth')), may hold values from 0 to 3584, as said below
- send_index: int32 [32, 8, 4, 512], P('plane', 'depth'), may hold values from 0 to 1023
- send_live: int32 [32, 8, 4], P('plane', 'depth'), may hold values from 128 to 512, as said below
- face_index: int32 [32, 8, 2, 256], P('plane', 'depth'), may hold values from 0 to 1023
Outputs:
- conductivity: float32 [64, 262144], P(None, ('plane', 'depth'))
- sensitivity: float32 [64, 262144], P(None, ('plane', 'depth'))
The draws below stay inside these ranges and needn't reach their ends.
Inputs may be any that keep to these rules, and one draw needn't show every extreme that they name: `links`: the slot 13 of every block names the block itself; column 3584 stands for a neighbour outside the design domain. `send_live`: every brick has one plane neighbour whose list is full.
All inputs are finite; a program needn't handle non-finite values.
Results may differ from the reference program's by a relative error of at most 0.0003.
Values sent between devices are 32-bit elements; how exact they have to be, the bound alone decides.
No kernel may reach another device: no remote copies, remote signals or barrier semaphores. Data moves between devices by JAX's collectives and lax.ppermute only.
A program may use at most 64 MiB of HBM per device.

```python
import math
import jax
import jax.numpy as jnp
from jax import lax

VOX = 64
KNB = 27
REACH = 2
CAP = 512
FACE = 256
BLK_DEV = 1024
GROUPS = 4
EXT = 3585
NB = 262144
N_PLANE = 32
N_DEPTH = 8


def draw_links(key, part):
    key = jax.random.fold_in(key, 11)
    key_pick, key_outside = jax.random.split(key)
    chosen = jax.random.randint(key_pick, (KNB, NB), 0, EXT - 1)
    outside = jax.random.randint(key_outside, (KNB, NB), 0, 8) == 0
    chosen = jnp.where(outside, EXT - 1, chosen)
    own_index = jnp.arange(NB, dtype=jnp.int32) % BLK_DEV
    centre = (jnp.arange(KNB) == KNB // 2)[:, None]
    return jnp.where(centre, own_index[None, :], chosen).astype(jnp.int32)


def draw_send_live(key, part):
    key = jax.random.fold_in(key, 23)
    key_count, key_full = jax.random.split(key)
    counted = jax.random.randint(key_count, (N_PLANE, N_DEPTH, GROUPS), CAP // 4, CAP + 1)
    fullest = jax.random.randint(key_full, (N_PLANE, N_DEPTH, 1), 0, GROUPS)
    member = jnp.arange(GROUPS)[None, None, :]
    first_brick = (jnp.arange(N_PLANE)[:, None, None] == 0) & (jnp.arange(N_DEPTH)[None, :, None] == 0)
    lowest = first_brick & (member == (fullest + 1) % GROUPS)
    counted = jnp.where(lowest, CAP // 4, counted)
    return jnp.where(member == fullest, CAP, counted).astype(jnp.int32)


def with_ends(values, rng, least, top_value):
    dims = values.shape
    spot = [jax.random.randint(jax.random.fold_in(rng, axis), (), 0, dims[axis]) for axis in range(len(dims))]
    values = values.at[tuple(spot)].set(least)
    longest = dims.index(max(dims))
    spot[longest] = (spot[longest] + 1) % dims[longest]
    return values.at[tuple(spot)].set(top_value)


def block_scale(stream_key, shape, shards, least, top_value):
    level = 1.0
    for axis_at, blocks in shards:
        heights = jax.random.uniform(jax.random.fold_in(jax.random.fold_in(stream_key, 6), axis_at), (blocks,), jnp.float32, least / len(shards), top_value / len(shards))
        level = level * jnp.repeat(jnp.exp(heights), shape[axis_at] // blocks).reshape((-1,) + (1,) * (len(shape) - 1 - axis_at))
    return level


def setup_inputs(seed: int = 0) -> dict:
    key_of = jax.random.split(jax.random.key(seed), 7)
    return {
        "density": jnp.clip(0.01 + 0.99 * jax.random.uniform(key_of[0], (VOX, NB), jnp.float32) ** block_scale(key_of[0], (VOX, NB), ((1, 256),), -0.2, 0.2), 0.01, 1.0),
        "energy": jnp.clip(jnp.exp(math.log(10.0) - 4.6051702 * jax.random.uniform(key_of[1], (VOX, NB), jnp.float32) ** block_scale(key_of[1], (VOX, NB), ((1, 256),), -0.2, 0.2)), 0.1, 10.0),
        "links": draw_links(jax.random.fold_in(key_of[6], 71), 0),
        "send_index": with_ends(jax.random.randint(key_of[3], (N_PLANE, N_DEPTH, GROUPS, CAP), 0, BLK_DEV), jax.random.fold_in(key_of[3], 1), 0, BLK_DEV - 1).astype(jnp.int32),
        "send_live": draw_send_live(jax.random.fold_in(key_of[6], 71), 0),
        "face_index": with_ends(jax.random.randint(key_of[5], (N_PLANE, N_DEPTH, 2, FACE), 0, BLK_DEV), jax.random.fold_in(key_of[5], 1), 0, BLK_DEV - 1).astype(jnp.int32),
    }


radius = 3.0
floor_value = 0.001
penalty = 3.0

def cone_table():
    voxels = jnp.arange(64)
    places = jnp.stack([voxels // 16, voxels // 4 % 4, voxels % 4], axis=-1).astype(jnp.float32)
    slots = jnp.arange(27)
    moved = jnp.stack([slots // 9 - 1, slots // 3 % 3 - 1, slots % 3 - 1], axis=-1).astype(jnp.float32) * 4.0
    apart = places[None, :, None, :] - places[None, None, :, :] - moved[:, None, None, :]
    return jnp.maximum(0.0, radius - jnp.sqrt(lax.optimization_barrier(jnp.sum(apart * apart, axis=-1))))

def local_pass(extended, link_table, energy_block, table):
    width = extended.shape[1]
    blocks = link_table.shape[1]
    row_sums = lax.optimization_barrier(jnp.sum(table, axis=2))
    valid = (link_table != width - 1).astype(jnp.float32)
    weight_sum = jnp.dot(row_sums.T, valid, precision=lax.Precision.HIGHEST)
    filtered = jnp.zeros((64, blocks), jnp.float32)
    for third in range(3):
        part_links = link_table[9 * third:9 * third + 9].reshape(-1)
        picked = jnp.take(extended, part_links, axis=1).reshape(64, 9, blocks)
        filtered = filtered + jnp.einsum('kij,jkb->ib', table[9 * third:9 * third + 9], picked, precision=lax.Precision.HIGHEST)
    filtered = filtered / weight_sum
    conductivity = floor_value + filtered * filtered * filtered * (1.0 - floor_value)
    scaled = -penalty * (1.0 - floor_value) * filtered * filtered * energy_block / weight_sum
    back = jnp.zeros((64, width), jnp.float32)
    for third in range(3):
        part_links = link_table[9 * third:9 * third + 9].reshape(-1)
        spread = jnp.einsum('kji,jb->ikb', table[9 * third:9 * third + 9], scaled, precision=lax.Precision.HIGHEST)
        back = back.at[:, part_links].add(spread.reshape(64, 9 * blocks))
    return (conductivity, back)

def reference(density, energy, links, send_index, send_live, face_index):
    table = cone_table()
    planes = N_PLANE
    depths = N_DEPTH

    def split(array, rows):
        return array.reshape(rows, planes, depths, BLK_DEV).transpose(1, 2, 0, 3)
    dens = split(density, 64)
    energies = split(energy, 64)
    link_parts = split(links, KNB)
    keep = (jnp.arange(CAP)[None, None, None, :] < send_live[..., None]).astype(jnp.float32)
    take_cols = jax.vmap(jax.vmap(lambda block, index: jnp.take(block, index, axis=1)))
    payload = take_cols(dens, send_index) * keep[:, :, None]
    offsets = [offset for offset in range(-REACH, REACH + 1) if offset != 0]
    padded = jnp.pad(payload, ((REACH, REACH), (0, 0), (0, 0), (0, 0), (0, 0)))
    received = [padded[REACH - offset:REACH - offset + planes, :, :, member] for member, offset in enumerate(offsets)]
    faces = take_cols(dens, face_index)
    face_pad = jnp.pad(faces, ((0, 0), (1, 1), (0, 0), (0, 0), (0, 0)))
    from_low = face_pad[:, 0:depths, :, 1]
    from_high = face_pad[:, 2:depths + 2, :, 0]
    extended = jnp.concatenate([dens] + received + [from_low, from_high, jnp.zeros((planes, depths, 64, 1), jnp.float32)], axis=3)
    width = extended.shape[3]

    def per_brick(items):
        return local_pass(items[0], items[1], items[2], table)
    cond_all, back_all = lax.map(per_brick, (extended.reshape(planes * depths, 64, width), link_parts.reshape(planes * depths, KNB, BLK_DEV), energies.reshape(planes * depths, 64, BLK_DEV)))
    cond_all = cond_all.reshape(planes, depths, 64, BLK_DEV)
    back_all = back_all.reshape(planes, depths, 64, width)
    sens = back_all[..., :BLK_DEV]
    values = []
    places = []
    for member, offset in enumerate(offsets):
        start = BLK_DEV + member * CAP
        piece = back_all[..., start:start + CAP]
        piece_pad = jnp.pad(piece, ((REACH, REACH), (0, 0), (0, 0), (0, 0)))
        returned = piece_pad[REACH + offset:REACH + offset + planes]
        values.append(returned * keep[:, :, None, member])
        places.append(send_index[:, :, member])
    low_start = BLK_DEV + len(offsets) * CAP
    low_back = back_all[..., low_start:low_start + FACE]
    high_back = back_all[..., low_start + FACE:low_start + 2 * FACE]
    low_pad = jnp.pad(low_back, ((0, 0), (1, 1), (0, 0), (0, 0)))
    high_pad = jnp.pad(high_back, ((0, 0), (1, 1), (0, 0), (0, 0)))
    values.append(high_pad[:, 0:depths])
    places.append(face_index[:, :, 0])
    values.append(low_pad[:, 2:depths + 2])
    places.append(face_index[:, :, 1])
    all_values = jnp.concatenate(values, axis=3)
    all_places = jnp.concatenate(places, axis=2)
    add_cols = jax.vmap(jax.vmap(lambda target, index, amount: target.at[:, index].add(amount)))
    sens = add_cols(sens, all_places, all_values)
    conductivity = cond_all.transpose(2, 0, 1, 3).reshape(64, NB)
    sensitivity = sens.transpose(2, 0, 1, 3).reshape(64, NB)
    return (conductivity, sensitivity)
```

```python
import jax
import jax.numpy as jnp
import numpy as np
from jax import lax
from jax.experimental import pallas as pl
from jax.experimental.pallas import tpu as pltpu
from jax.sharding import PartitionSpec as P

REACH = 2
TILE = 256
radius = 3.0
floor_value = 0.001
penalty = 3.0

F32 = jnp.float32
BF16 = jnp.bfloat16

ORDERS = ((0, 1, 2), (2, 0, 1), (1, 2, 0))


def cone_table():
    voxels = np.arange(64)
    places = np.stack([voxels // 16, voxels // 4 % 4, voxels % 4], axis=-1)
    slots = np.arange(27)
    moved = np.stack([slots // 9 - 1, slots // 3 % 3 - 1, slots % 3 - 1], axis=-1) * 4
    apart = places[None, :, None, :] - places[None, None, :, :] - moved[:, None, None, :]
    squares = np.sum(apart * apart, axis=-1).astype(np.float32)
    return np.maximum(np.float32(0.0), np.float32(radius) - np.sqrt(squares))


def order_voxels(order):
    rows = np.arange(64)
    coords = np.zeros((3, 64), np.int64)
    coords[order[0]], coords[order[1]], coords[order[2]] = rows // 16, rows // 4 % 4, rows % 4
    return coords[0] * 16 + coords[1] * 4 + coords[2]


def slot_of(offset):
    return (offset[0] + 1) * 9 + (offset[1] + 1) * 3 + offset[2] + 1


def layout():
    faces, edges, corners = [], [], []
    for at, order in enumerate(ORDERS):
        for sign in (-1, 1):
            offset = [0, 0, 0]
            offset[order[0]] = sign
            faces.append((slot_of(offset), at, sign))
    for at, order in enumerate(ORDERS):
        for one in (-1, 1):
            for two in (-1, 1):
                offset = [0, 0, 0]
                offset[order[0]], offset[order[1]] = one, two
                edges.append((slot_of(offset), at, one, two))
    for a in (-1, 1):
        for b in (-1, 1):
            for c in (-1, 1):
                corners.append(slot_of((a, b, c)))
    return faces, edges, corners


FACES, EDGES, CORNERS = layout()
SLOTS = [f[0] for f in FACES] + [e[0] for e in EDGES] + CORNERS


def face_start(sign, forward):
    return 32 if (sign > 0) == forward else 0


def edge_starts(one, two, forward):
    first = 2 if (one > 0) == forward else 0
    second = 2 if (two > 0) == forward else 0
    return [(first + i) * 16 + second * 4 for i in range(2)]


def slot_rows(forward):
    voxels = [order_voxels(order) for order in ORDERS]
    out = []
    for slot, at, sign in FACES:
        start = face_start(sign, forward)
        out.append((slot, voxels[at][start : start + 32]))
    for slot, at, one, two in EDGES:
        rows = np.concatenate([voxels[at][s : s + 8] for s in edge_starts(one, two, forward)])
        out.append((slot, rows))
    return out


def pieces_np(table):
    high = table.astype(jnp.bfloat16)
    low = (table - high.astype(np.float32)).astype(jnp.bfloat16)
    return high, low


def three(table):
    high, low = pieces_np(table)
    return np.concatenate([high, low, high], axis=1)


def corner_rows(table, forward):
    out = []
    for slot in CORNERS:
        part = table[slot] if forward else table[slot].T
        counts = (part > 0).sum(axis=1)
        main = int(np.argmax(counts))
        rest = [int(v) for v in np.nonzero(counts)[0] if v != main]
        out.append((part, main, rest))
    return out


def constants():
    table = cone_table()
    fold_fwd = [table[slot][rows] for slot, rows in slot_rows(True)]
    fold_bwd = [table[slot].T[rows] for slot, rows in slot_rows(False)]
    cor_fwd, cor_bwd = corner_rows(table, True), corner_rows(table, False)
    fold_fwd += [np.stack([part[main] for part, main, rest in cor_fwd])]
    fold_fwd += [np.stack([part[rest[0]] for part, main, rest in cor_fwd])]
    for part, main, rest in cor_bwd:
        fold_bwd += [np.tile(np.stack([part[main], part[rest[0]]]), (8, 1))]
    spots = []
    for at in (1, 2):
        spot = np.zeros((64, 64), np.float32)
        spot[order_voxels(ORDERS[at]), np.arange(64)] = 1
        spots.append(spot)
    cf = np.zeros((64, 16), np.float32)
    for m, (part, main, rest) in enumerate(cor_fwd):
        cf[main, m] = 1
        cf[rest, 8 + m] = 1
    join_fwd = np.concatenate(spots + [cf], axis=1)
    join_fwd = np.concatenate([join_fwd, join_fwd], axis=1).astype(jnp.bfloat16)
    joins = []
    for parity in range(2):
        cb = np.zeros((64, 64), np.float32)
        for m, (part, main, rest) in enumerate(cor_bwd):
            for piece in range(2):
                cb[main, m * 8 + parity * 4 + piece * 2] = 1
                cb[rest, m * 8 + parity * 4 + piece * 2 + 1] = 1
        join = np.concatenate(spots + [cb], axis=1)
        joins.append(np.concatenate([join, join], axis=1))
    sums = table.sum(axis=2).T
    high, low = pieces_np(sums)
    return dict(
        fold_fwd=three(np.concatenate(fold_fwd)),
        fold_bwd=three(np.concatenate(fold_bwd)),
        own=three(table[13]),
        own_t=three(table[13].T),
        join_fwd=join_fwd,
        join_bwd=np.concatenate(joins).astype(jnp.bfloat16),
        sums=np.concatenate([high, low], axis=1),
    )


def split2(value):
    high = value.astype(BF16)
    return high, (value - high.astype(F32)).astype(BF16)


def pieces(value):
    high, low = split2(value)
    return jnp.concatenate([high, high, low], axis=0)


def dot(a, b):
    return jnp.dot(a, b, preferred_element_type=F32)


def dot_nt(a, b):
    return lax.dot_general(a, b, (((1,), (1,)), ((), ())), preferred_element_type=F32)


def one_hot(low):
    shape = (TILE, low.shape[1])
    hit = lax.broadcasted_iota(jnp.int32, shape, 0) == jnp.broadcast_to(low, shape)
    return hit.astype(F32).astype(BF16)


def order_links(links_ref, rows_ref):
    for at, slot in enumerate(SLOTS):
        rows_ref[at : at + 1, :] = links_ref[slot : slot + 1, :]


def gather_filtered(chunks, first, rows_ref, fold_ref, join_ref, tf, te, yc, pf, pe):
    count = len(chunks)
    faces, edges = len(FACES), len(EDGES)
    blocks = rows_ref.shape[1]
    for h, chunk in enumerate(chunks):
        y = dot(fold_ref[...], pieces(chunk))
        high, low = split2(y[:384])
        for f in range(faces):
            tf[f, h * 32 : h * 32 + 32, 0:TILE] = high[f * 32 : f * 32 + 32]
            tf[f, h * 32 : h * 32 + 32, TILE : 2 * TILE] = low[f * 32 : f * 32 + 32]
        for e in range(edges):
            at = 192 + e * 16
            te[e, h * 16 : h * 16 + 16, 0:TILE] = high[at : at + 16]
            te[e, h * 16 : h * 16 + 16, TILE : 2 * TILE] = low[at : at + 16]
        yc[:, h * TILE : h * TILE + TILE] = y[384:400]

    def make(table, out, rows, base):
        def step(s, carry):
            for nb in range(blocks // TILE):
                cols = slice(nb * TILE, nb * TILE + TILE)
                idx = rows_ref[pl.ds(base + s, 1), cols]
                hot = one_hot(idx & (TILE - 1))
                upper = jnp.broadcast_to((idx >> 8) - first, (rows, TILE))
                got = dot(table[s, :, 0:TILE], hot) + dot(table[s, :, TILE : 2 * TILE], hot)
                acc = jnp.zeros((rows, TILE), F32)
                for h in range(count):
                    acc = jnp.where(upper == h, got[h * rows : h * rows + rows], acc)
                out[s, :, cols] = acc
            return carry

        return step

    lax.fori_loop(0, faces, make(tf, pf, 32, 0), 0)
    lax.fori_loop(0, edges, make(te, pe, 16, faces), 0)
    corner = [[], []]
    for bg in range(blocks // 128):
        idx = rows_ref[18:26, bg * 128 : bg * 128 + 128]
        low, upper = idx & 127, (idx >> 7) - 2 * first
        acc = [jnp.zeros((8, 128), F32), jnp.zeros((8, 128), F32)]
        for h in range(2 * count):
            hit = upper == h
            for c in range(2):
                got = jnp.take_along_axis(yc[c * 8 : c * 8 + 8, h * 128 : h * 128 + 128], low, axis=1)
                acc[c] = jnp.where(hit, got, acc[c])
        for c in range(2):
            corner[c].append(acc[c])
    corner = [jnp.concatenate(c, axis=1) for c in corner]
    totals = order_totals(lambda f: pf[f], lambda e: pe[e], True)
    high, low = split2(jnp.concatenate([totals[1], totals[2]] + corner, axis=0))
    return totals[0] + dot(join_ref[...], jnp.concatenate([high, low], axis=0))


def order_totals(face, edge, forward):
    totals = []
    for at in range(3):
        runs = [None] * 8
        for f, (_, order, sign) in enumerate(FACES):
            if order == at:
                value, start = face(f), face_start(sign, forward)
                for i in range(4):
                    runs[start // 8 + i] = value[i * 8 : i * 8 + 8]
        for e, (_, order, one, two) in enumerate(EDGES):
            if order == at:
                value = edge(e)
                for i, start in enumerate(edge_starts(one, two, forward)):
                    runs[start // 8] = runs[start // 8] + value[i * 8 : i * 8 + 8]
        totals.append(jnp.concatenate(runs, axis=0))
    return totals


def scatter_back(scaled, first, count, rows_ref, fold_ref, join_ref, sf, se, sc, zf, ze, zc):
    faces, edges, corners = len(FACES), len(EDGES), len(CORNERS)
    blocks = rows_ref.shape[1]
    spread = dot(fold_ref[...], pieces(scaled))
    high, low = split2(spread)
    for f in range(faces):
        sf[f, 0:32, :] = high[f * 32 : f * 32 + 32]
        sf[f, 32:64, :] = low[f * 32 : f * 32 + 32]
    for e in range(edges):
        at = 192 + e * 16
        se[e, 0:16, :] = high[at : at + 16]
        se[e, 16:32, :] = low[at : at + 16]
    is_high = lax.broadcasted_iota(jnp.int32, (16, blocks), 0) % 4 < 2
    for m in range(corners):
        part = spread[384 + m * 16 : 384 + m * 16 + 16]
        top = part.astype(BF16).astype(F32)
        sc[m, :, :] = jnp.where(is_high, top, part - top).astype(BF16)

    def make(values, out, rows, base):
        def step(s, carry):
            idx = rows_ref[pl.ds(base + s, 1), :]
            hot = one_hot(idx & (TILE - 1))
            upper = (idx >> 8) - first
            value = values[s]
            parts = [value * (upper == h).astype(F32).astype(BF16) for h in range(count)]
            got = dot_nt(jnp.concatenate(parts, axis=0), hot)
            for h in range(count):
                at = h * 2 * rows
                out[s, h * rows : h * rows + rows, :] = got[at : at + rows] + got[at + rows : at + 2 * rows]
            return carry

        return step

    lax.fori_loop(0, faces, make(sf, zf, 32, 0), 0)
    lax.fori_loop(0, edges, make(se, ze, 16, faces), 0)
    fours = (count + 3) // 4

    def corner_step(m, carry):
        idx = rows_ref[pl.ds(18 + m, 1), :]
        hot = one_hot(idx & (TILE - 1))
        upper = jnp.broadcast_to((idx >> 8) - first, (16, blocks))
        quarter = lax.broadcasted_iota(jnp.int32, (16, blocks), 0) // 4
        value = sc[m]
        parts = [
            value * (upper == quarter + 4 * q).astype(F32).astype(BF16) for q in range(fours)
        ]
        zc[m, :, :] = dot_nt(jnp.concatenate(parts, axis=0), hot)
        return carry

    lax.fori_loop(0, corners, corner_step, 0)
    out = []
    for h in range(count):
        totals = order_totals(
            lambda f: zf[f, h * 32 : h * 32 + 32, :], lambda e: ze[e, h * 16 : h * 16 + 16, :], False
        )
        at = h // 2 * 8
        tops = [zc[m, at : at + 8, :] for m in range(corners)]
        high, low = split2(jnp.concatenate([totals[1], totals[2]] + tops, axis=0))
        join = join_ref[h % 2 * 64 : h % 2 * 64 + 64, :]
        out.append(totals[0] + dot(join, jnp.concatenate([high, low], axis=0)))
    return out


def payload_kernel(live_ref, density_ref, index_ref, face_ref, *outs):
    density = density_ref[...]
    high, low = split2(density)
    heads = density.shape[1] // TILE
    table = jnp.concatenate(
        [
            jnp.concatenate([p[:, h * TILE : h * TILE + TILE] for h in range(heads)], axis=0)
            for p in (high, low)
        ],
        axis=1,
    )

    def pick(idx, upper):
        hot = one_hot(idx & (TILE - 1))
        got = dot(table[:, 0:TILE], hot) + dot(table[:, TILE : 2 * TILE], hot)
        upper = jnp.broadcast_to(upper, (64, idx.shape[1]))
        acc = jnp.zeros((64, idx.shape[1]), F32)
        for h in range(heads):
            acc = jnp.where(upper == h, got[h * 64 : h * 64 + 64], acc)
        return acc

    groups = index_ref.shape[0]
    for g in range(groups):
        idx = index_ref[g : g + 1, :]
        at = lax.broadcasted_iota(jnp.int32, idx.shape, 1)
        outs[g][...] = pick(idx, jnp.where(at < live_ref[g], idx >> 8, -1))
    for side in range(2):
        idx = face_ref[side : side + 1, :]
        outs[groups + side][...] = pick(idx, idx >> 8)


def local_kernel(
    density_ref, links_ref, fold_ref, join_ref, own_ref, sums_ref, part_ref, weight_ref, rows_ref, *scratch
):
    order_links(links_ref, rows_ref)
    density = density_ref[...]
    heads = density.shape[1] // TILE
    chunks = [density[:, h * TILE : h * TILE + TILE] for h in range(heads)]
    part = gather_filtered(chunks, 0, rows_ref, fold_ref, join_ref, *scratch)
    part_ref[...] = part + dot(own_ref[...], pieces(density))
    valid = (links_ref[...] != 14 * TILE).astype(F32).astype(BF16)
    weight_ref[...] = dot(sums_ref[...], jnp.concatenate([valid, valid], axis=0))


def remote_kernel(
    r0, r1, r2, r3, low_ref, high_ref, links_ref, part_ref, weight_ref, energy_ref,
    fold_ref, join_ref, fold_b_ref, join_b_ref,
    cond_ref, scaled_ref, b0, b1, b2, b3, lb, ub, rows_ref, *scratch,
):
    order_links(links_ref, rows_ref)
    chunks = []
    for ref in (r0, r1, r2, r3, low_ref, high_ref):
        for at in range(0, ref.shape[1], TILE):
            chunks.append(ref[:, at : at + TILE])
    total = gather_filtered(chunks, 4, rows_ref, fold_ref, join_ref, *scratch[:5])
    weight = weight_ref[...]
    filtered = (part_ref[...] + total) / weight
    square = filtered * filtered
    cond_ref[...] = floor_value + square * filtered * (1.0 - floor_value)
    scaled = -penalty * (1.0 - floor_value) * square * energy_ref[...] / weight
    scaled_ref[...] = scaled
    back = scatter_back(scaled, 4, len(chunks), rows_ref, fold_b_ref, join_b_ref, *scratch[5:])
    at = 0
    for ref in (b0, b1, b2, b3, lb, ub):
        for start in range(0, ref.shape[1], TILE):
            ref[:, start : start + TILE] = back[at]
            at += 1


def own_kernel(scaled_ref, links_ref, fold_b_ref, join_b_ref, own_ref, sens_ref, rows_ref, *scratch):
    order_links(links_ref, rows_ref)
    scaled = scaled_ref[...]
    heads = scaled.shape[1] // TILE
    back = scatter_back(scaled, 0, heads, rows_ref, fold_b_ref, join_b_ref, *scratch)
    sens_ref[...] = jnp.concatenate(back, axis=1) + dot(own_ref[...], pieces(scaled))


def final_kernel(live_ref, sens_ref, index_ref, face_ref, v0, v1, v2, v3, v4, v5, out_ref):
    heads = sens_ref.shape[1] // TILE
    groups = index_ref.shape[0]
    total = jnp.zeros((heads * 128, TILE), F32)
    for g, ref in enumerate((v0, v1, v2, v3, v4, v5)):
        if g < groups:
            idx = index_ref[g : g + 1, :]
            at = lax.broadcasted_iota(jnp.int32, idx.shape, 1)
            upper = jnp.where(at < live_ref[g], idx >> 8, -1)
        else:
            idx = face_ref[g - groups : g - groups + 1, :]
            upper = idx >> 8
        hot = one_hot(idx & (TILE - 1))
        value = jnp.concatenate(split2(ref[...]), axis=0)
        parts = [value * (upper == h).astype(F32).astype(BF16) for h in range(heads)]
        total = total + dot_nt(jnp.concatenate(parts, axis=0), hot)
    for h in range(heads):
        cols = slice(h * TILE, h * TILE + TILE)
        both = total[h * 128 : h * 128 + 64] + total[h * 128 + 64 : h * 128 + 128]
        out_ref[:, cols] = sens_ref[:, cols] + both


def params():
    return pltpu.CompilerParams(vmem_limit_bytes=48 * 1024 * 1024)


def cost(us):
    return pl.CostEstimate(flops=int(us * 5e8), bytes_accessed=int(us * 2e6), transcendentals=0)


def gather_scratch(count, blocks):
    return [
        pltpu.VMEM((6, count * 32, 2 * TILE), BF16),
        pltpu.VMEM((12, count * 16, 2 * TILE), BF16),
        pltpu.VMEM((16, count * TILE), F32),
        pltpu.VMEM((6, 32, blocks), F32),
        pltpu.VMEM((12, 16, blocks), F32),
    ]


def scatter_scratch(count, blocks):
    return [
        pltpu.VMEM((6, 64, blocks), BF16),
        pltpu.VMEM((12, 32, blocks), BF16),
        pltpu.VMEM((8, 16, blocks), BF16),
        pltpu.VMEM((6, count * 32, TILE), F32),
        pltpu.VMEM((12, count * 16, TILE), F32),
        pltpu.VMEM((8, (count + 3) // 4 * 16, TILE), F32),
    ]


def passed_along(shard, axis, by):
    count = lax.axis_size(axis)
    pairs = [(i, i + by) for i in range(count) if 0 <= i + by < count]
    return lax.ppermute(shard, axis, pairs)


def on_device(density, energy, links, send_index, send_live, face_index):
    const = {name: jnp.asarray(value) for name, value in constants().items()}
    blocks = density.shape[1]
    indices, counts, faces_at = send_index[0, 0], send_live[0, 0], face_index[0, 0]
    capacity, face_count = indices.shape[1], faces_at.shape[1]
    whole = jax.ShapeDtypeStruct((64, blocks), F32)
    listed = jax.ShapeDtypeStruct((64, capacity), F32)
    faced = jax.ShapeDtypeStruct((64, face_count), F32)
    vmem = pl.BlockSpec(memory_space=pltpu.VMEM)
    smem = pl.BlockSpec(memory_space=pltpu.SMEM)
    ordered = pltpu.VMEM((32, blocks), jnp.int32)
    offsets = [offset for offset in range(-REACH, REACH + 1) if offset != 0]

    loads = pl.pallas_call(
        payload_kernel,
        out_shape=[listed] * 4 + [faced] * 2,
        in_specs=[smem, vmem, vmem, vmem],
        out_specs=[vmem] * 6,
        compiler_params=params(),
        cost_estimate=cost(3),
    )(counts, density, indices, faces_at)
    received = [passed_along(loads[m], "plane", offset) for m, offset in enumerate(offsets)]
    from_low = passed_along(loads[5], "depth", 1)
    from_high = passed_along(loads[4], "depth", -1)
    part, weight = pl.pallas_call(
        local_kernel,
        out_shape=[whole, whole],
        in_specs=[vmem] * 6,
        out_specs=[vmem] * 2,
        scratch_shapes=[ordered] + gather_scratch(4, blocks),
        compiler_params=params(),
        cost_estimate=cost(8),
    )(density, links, const["fold_fwd"], const["join_fwd"], const["own"], const["sums"])
    conductivity, scaled, *groups_back = pl.pallas_call(
        remote_kernel,
        out_shape=[whole, whole] + [listed] * 4 + [faced] * 2,
        in_specs=[vmem] * 14,
        out_specs=[vmem] * 8,
        scratch_shapes=[ordered] + gather_scratch(10, blocks) + scatter_scratch(10, blocks),
        compiler_params=params(),
        cost_estimate=cost(20),
    )(
        *received, from_low, from_high, links, part, weight, energy,
        const["fold_fwd"], const["join_fwd"], const["fold_bwd"], const["join_bwd"],
    )
    returned = [passed_along(groups_back[m], "plane", -offset) for m, offset in enumerate(offsets)]
    to_one = passed_along(groups_back[4], "depth", -1)
    to_zero = passed_along(groups_back[5], "depth", 1)
    sens = pl.pallas_call(
        own_kernel,
        out_shape=whole,
        in_specs=[vmem] * 5,
        out_specs=vmem,
        scratch_shapes=[ordered] + scatter_scratch(4, blocks),
        compiler_params=params(),
        cost_estimate=cost(8),
    )(scaled, links, const["fold_bwd"], const["join_bwd"], const["own_t"])
    sens = pl.pallas_call(
        final_kernel,
        out_shape=whole,
        in_specs=[smem] + [vmem] * 9,
        out_specs=vmem,
        compiler_params=params(),
        cost_estimate=cost(3),
    )(counts, sens, indices, faces_at, *returned, to_zero, to_one)
    return (conductivity, sens)


def solution(mesh):
    in_specs = (
        P(None, ("plane", "depth")),
        P(None, ("plane", "depth")),
        P(None, ("plane", "depth")),
        P("plane", "depth", None, None),
        P("plane", "depth", None),
        P("plane", "depth", None, None),
    )
    out_specs = (P(None, ("plane", "depth")), P(None, ("plane", "depth")))
    return jax.shard_map(
        on_device, mesh=mesh, in_specs=in_specs, out_specs=out_specs, check_vma=False
    )
```

```python
import jax
import jax.numpy as jnp
import numpy as np
from jax import lax
from jax.experimental import pallas as pl
from jax.experimental.pallas import tpu as pltpu
from jax.sharding import PartitionSpec as P

REACH = 2
TILE = 256
radius = 3.0
floor_value = 0.001
penalty = 3.0

F32 = jnp.float32
BF16 = jnp.bfloat16

ORDERS = ((0, 1, 2), (2, 0, 1), (1, 2, 0))


def cone_table():
    voxels = np.arange(64)
    places = np.stack([voxels // 16, voxels // 4 % 4, voxels % 4], axis=-1)
    slots = np.arange(27)
    moved = np.stack([slots // 9 - 1, slots // 3 % 3 - 1, slots % 3 - 1], axis=-1) * 4
    apart = places[None, :, None, :] - places[None, None, :, :] - moved[:, None, None, :]
    squares = np.sum(apart * apart, axis=-1).astype(np.float32)
    return np.maximum(np.float32(0.0), np.float32(radius) - np.sqrt(squares))


def order_voxels(order):
    rows = np.arange(64)
    coords = np.zeros((3, 64), np.int64)
    coords[order[0]], coords[order[1]], coords[order[2]] = rows // 16, rows // 4 % 4, rows % 4
    return coords[0] * 16 + coords[1] * 4 + coords[2]


def slot_of(offset):
    return (offset[0] + 1) * 9 + (offset[1] + 1) * 3 + offset[2] + 1


def layout():
    faces, edges, corners = [], [], []
    for at, order in enumerate(ORDERS):
        for sign in (-1, 1):
            offset = [0, 0, 0]
            offset[order[0]] = sign
            faces.append((slot_of(offset), at, sign))
    for at, order in enumerate(ORDERS):
        for one in (-1, 1):
            for two in (-1, 1):
                offset = [0, 0, 0]
                offset[order[0]], offset[order[1]] = one, two
                edges.append((slot_of(offset), at, one, two))
    for a in (-1, 1):
        for b in (-1, 1):
            for c in (-1, 1):
                corners.append(slot_of((a, b, c)))
    return faces, edges, corners


FACES, EDGES, CORNERS = layout()
SLOTS = [f[0] for f in FACES] + [e[0] for e in EDGES] + CORNERS


def face_start(sign, forward):
    return 32 if (sign > 0) == forward else 0


def edge_starts(one, two, forward):
    first = 2 if (one > 0) == forward else 0
    second = 2 if (two > 0) == forward else 0
    return [(first + i) * 16 + second * 4 for i in range(2)]


def slot_rows(forward):
    voxels = [order_voxels(order) for order in ORDERS]
    out = []
    for slot, at, sign in FACES:
        start = face_start(sign, forward)
        out.append((slot, voxels[at][start : start + 32]))
    for slot, at, one, two in EDGES:
        rows = np.concatenate([voxels[at][s : s + 8] for s in edge_starts(one, two, forward)])
        out.append((slot, rows))
    return out


def pieces_np(table):
    high = table.astype(jnp.bfloat16)
    low = (table - high.astype(np.float32)).astype(jnp.bfloat16)
    return high, low


def three(table):
    high, low = pieces_np(table)
    return np.concatenate([high, low, high], axis=1)


def corner_rows(table, forward):
    out = []
    for slot in CORNERS:
        part = table[slot] if forward else table[slot].T
        counts = (part > 0).sum(axis=1)
        main = int(np.argmax(counts))
        rest = [int(v) for v in np.nonzero(counts)[0] if v != main]
        out.append((part, main, rest))
    return out


def constants():
    table = cone_table()
    fold_fwd = [table[slot][rows] for slot, rows in slot_rows(True)]
    fold_bwd = [table[slot].T[rows] for slot, rows in slot_rows(False)]
    cor_fwd, cor_bwd = corner_rows(table, True), corner_rows(table, False)
    fold_fwd += [np.stack([part[main] for part, main, rest in cor_fwd])]
    fold_fwd += [np.stack([part[rest[0]] for part, main, rest in cor_fwd])]
    for part, main, rest in cor_bwd:
        fold_bwd += [np.tile(np.stack([part[main], part[rest[0]]]), (8, 1))]
    spots = []
    for at in (1, 2):
        spot = np.zeros((64, 64), np.float32)
        spot[order_voxels(ORDERS[at]), np.arange(64)] = 1
        spots.append(spot)
    cf = np.zeros((64, 16), np.float32)
    for m, (part, main, rest) in enumerate(cor_fwd):
        cf[main, m] = 1
        cf[rest, 8 + m] = 1
    join_fwd = np.concatenate(spots + [cf], axis=1)
    join_fwd = np.concatenate([join_fwd, join_fwd], axis=1).astype(jnp.bfloat16)
    joins = []
    for parity in range(2):
        cb = np.zeros((64, 64), np.float32)
        for m, (part, main, rest) in enumerate(cor_bwd):
            for piece in range(2):
                cb[main, m * 8 + parity * 4 + piece * 2] = 1
                cb[rest, m * 8 + parity * 4 + piece * 2 + 1] = 1
        join = np.concatenate(spots + [cb], axis=1)
        joins.append(np.concatenate([join, join], axis=1))
    sums = table.sum(axis=2).T
    high, low = pieces_np(sums)
    return dict(
        fold_fwd=three(np.concatenate(fold_fwd)),
        fold_bwd=three(np.concatenate(fold_bwd)),
        own=three(table[13]),
        own_t=three(table[13].T),
        join_fwd=join_fwd,
        join_bwd=np.concatenate(joins).astype(jnp.bfloat16),
        sums=np.concatenate([high, low], axis=1),
    )


def split2(value):
    high = value.astype(BF16)
    return high, (value - high.astype(F32)).astype(BF16)


def pieces(value):
    high, low = split2(value)
    return jnp.concatenate([high, high, low], axis=0)


def dot(a, b):
    return jnp.dot(a, b, preferred_element_type=F32)


def dot_nt(a, b):
    return lax.dot_general(a, b, (((1,), (1,)), ((), ())), preferred_element_type=F32)


def one_hot(low):
    shape = (TILE, low.shape[1])
    hit = lax.broadcasted_iota(jnp.int32, shape, 0) == jnp.broadcast_to(low, shape)
    return hit.astype(F32).astype(BF16)


def order_links(links_ref, rows_ref):
    for at, slot in enumerate(SLOTS):
        rows_ref[at : at + 1, :] = links_ref[slot : slot + 1, :]


def gather_filtered(chunks, first, rows_ref, fold_ref, join_ref, tf, te, yc, pf, pe):
    count = len(chunks)
    faces, edges = len(FACES), len(EDGES)
    blocks = rows_ref.shape[1]
    for h, chunk in enumerate(chunks):
        y = dot(fold_ref[...], pieces(chunk))
        high, low = split2(y[:384])
        for f in range(faces):
            tf[f, h * 32 : h * 32 + 32, 0:TILE] = high[f * 32 : f * 32 + 32]
            tf[f, h * 32 : h * 32 + 32, TILE : 2 * TILE] = low[f * 32 : f * 32 + 32]
        for e in range(edges):
            at = 192 + e * 16
            te[e, h * 16 : h * 16 + 16, 0:TILE] = high[at : at + 16]
            te[e, h * 16 : h * 16 + 16, TILE : 2 * TILE] = low[at : at + 16]
        yc[:, h * TILE : h * TILE + TILE] = y[384:400]

    def make(table, out, rows, base):
        def step(s, carry):
            for nb in range(blocks // TILE):
                cols = slice(nb * TILE, nb * TILE + TILE)
                idx = rows_ref[pl.ds(base + s, 1), cols]
                hot = one_hot(idx & (TILE - 1))
                upper = jnp.broadcast_to((idx >> 8) - first, (rows, TILE))
                got = dot(table[s, :, 0:TILE], hot) + dot(table[s, :, TILE : 2 * TILE], hot)
                acc = jnp.zeros((rows, TILE), F32)
                for h in range(count):
                    acc = jnp.where(upper == h, got[h * rows : h * rows + rows], acc)
                out[s, :, cols] = acc
            return carry

        return step

    lax.fori_loop(0, faces, make(tf, pf, 32, 0), 0, unroll=True)
    lax.fori_loop(0, edges, make(te, pe, 16, faces), 0, unroll=True)
    corner = [[], []]
    for bg in range(blocks // 128):
        idx = rows_ref[18:26, bg * 128 : bg * 128 + 128]
        low, upper = idx & 127, (idx >> 7) - 2 * first
        acc = [jnp.zeros((8, 128), F32), jnp.zeros((8, 128), F32)]
        for h in range(2 * count):
            hit = upper == h
            for c in range(2):
                got = jnp.take_along_axis(yc[c * 8 : c * 8 + 8, h * 128 : h * 128 + 128], low, axis=1)
                acc[c] = jnp.where(hit, got, acc[c])
        for c in range(2):
            corner[c].append(acc[c])
    corner = [jnp.concatenate(c, axis=1) for c in corner]
    totals = order_totals(lambda f: pf[f], lambda e: pe[e], True)
    high, low = split2(jnp.concatenate([totals[1], totals[2]] + corner, axis=0))
    return totals[0] + dot(join_ref[...], jnp.concatenate([high, low], axis=0))


def order_totals(face, edge, forward):
    totals = []
    for at in range(3):
        runs = [None] * 8
        for f, (_, order, sign) in enumerate(FACES):
            if order == at:
                value, start = face(f), face_start(sign, forward)
                for i in range(4):
                    runs[start // 8 + i] = value[i * 8 : i * 8 + 8]
        for e, (_, order, one, two) in enumerate(EDGES):
            if order == at:
                value = edge(e)
                for i, start in enumerate(edge_starts(one, two, forward)):
                    runs[start // 8] = runs[start // 8] + value[i * 8 : i * 8 + 8]
        totals.append(jnp.concatenate(runs, axis=0))
    return totals


def scatter_back(scaled, first, count, rows_ref, fold_ref, join_ref, sf, se, sc, zf, ze, zc):
    faces, edges, corners = len(FACES), len(EDGES), len(CORNERS)
    blocks = rows_ref.shape[1]
    spread = dot(fold_ref[...], pieces(scaled))
    high, low = split2(spread)
    for f in range(faces):
        sf[f, 0:32, :] = high[f * 32 : f * 32 + 32]
        sf[f, 32:64, :] = low[f * 32 : f * 32 + 32]
    for e in range(edges):
        at = 192 + e * 16
        se[e, 0:16, :] = high[at : at + 16]
        se[e, 16:32, :] = low[at : at + 16]
    is_high = lax.broadcasted_iota(jnp.int32, (16, blocks), 0) % 4 < 2
    for m in range(corners):
        part = spread[384 + m * 16 : 384 + m * 16 + 16]
        top = part.astype(BF16).astype(F32)
        sc[m, :, :] = jnp.where(is_high, top, part - top).astype(BF16)

    def make(values, out, rows, base):
        def step(s, carry):
            idx = rows_ref[pl.ds(base + s, 1), :]
            hot = one_hot(idx & (TILE - 1))
            upper = (idx >> 8) - first
            value = values[s]
            parts = [value * (upper == h).astype(F32).astype(BF16) for h in range(count)]
            got = dot_nt(jnp.concatenate(parts, axis=0), hot)
            for h in range(count):
                at = h * 2 * rows
                out[s, h * rows : h * rows + rows, :] = got[at : at + rows] + got[at + rows : at + 2 * rows]
            return carry

        return step

    lax.fori_loop(0, faces, make(sf, zf, 32, 0), 0, unroll=True)
    lax.fori_loop(0, edges, make(se, ze, 16, faces), 0, unroll=True)
    fours = (count + 3) // 4

    def corner_step(m, carry):
        idx = rows_ref[pl.ds(18 + m, 1), :]
        hot = one_hot(idx & (TILE - 1))
        upper = jnp.broadcast_to((idx >> 8) - first, (16, blocks))
        quarter = lax.broadcasted_iota(jnp.int32, (16, blocks), 0) // 4
        value = sc[m]
        parts = [
            value * (upper == quarter + 4 * q).astype(F32).astype(BF16) for q in range(fours)
        ]
        zc[m, :, :] = dot_nt(jnp.concatenate(parts, axis=0), hot)
        return carry

    lax.fori_loop(0, corners, corner_step, 0, unroll=True)
    out = []
    for h in range(count):
        totals = order_totals(
            lambda f: zf[f, h * 32 : h * 32 + 32, :], lambda e: ze[e, h * 16 : h * 16 + 16, :], False
        )
        at = h // 2 * 8
        tops = [zc[m, at : at + 8, :] for m in range(corners)]
        high, low = split2(jnp.concatenate([totals[1], totals[2]] + tops, axis=0))
        join = join_ref[h % 2 * 64 : h % 2 * 64 + 64, :]
        out.append(totals[0] + dot(join, jnp.concatenate([high, low], axis=0)))
    return out


def payload_kernel(live_ref, density_ref, index_ref, face_ref, *outs):
    density = density_ref[...]
    high, low = split2(density)
    heads = density.shape[1] // TILE
    table = jnp.concatenate(
        [
            jnp.concatenate([p[:, h * TILE : h * TILE + TILE] for h in range(heads)], axis=0)
            for p in (high, low)
        ],
        axis=1,
    )

    def pick(idx, upper):
        hot = one_hot(idx & (TILE - 1))
        got = dot(table[:, 0:TILE], hot) + dot(table[:, TILE : 2 * TILE], hot)
        upper = jnp.broadcast_to(upper, (64, idx.shape[1]))
        acc = jnp.zeros((64, idx.shape[1]), F32)
        for h in range(heads):
            acc = jnp.where(upper == h, got[h * 64 : h * 64 + 64], acc)
        return acc

    groups = index_ref.shape[0]
    for g in range(groups):
        idx = index_ref[g : g + 1, :]
        at = lax.broadcasted_iota(jnp.int32, idx.shape, 1)
        outs[g][...] = pick(idx, jnp.where(at < live_ref[g], idx >> 8, -1))
    for side in range(2):
        idx = face_ref[side : side + 1, :]
        outs[groups + side][...] = pick(idx, jnp.where(live_ref[groups + side] > 0, idx >> 8, -1))


def local_kernel(
    density_ref, links_ref, fold_ref, join_ref, own_ref, sums_ref, part_ref, weight_ref, rows_ref, *scratch
):
    order_links(links_ref, rows_ref)
    density = density_ref[...]
    heads = density.shape[1] // TILE
    chunks = [density[:, h * TILE : h * TILE + TILE] for h in range(heads)]
    part = gather_filtered(chunks, 0, rows_ref, fold_ref, join_ref, *scratch)
    part_ref[...] = part + dot(own_ref[...], pieces(density))
    valid = (links_ref[...] != 14 * TILE).astype(F32).astype(BF16)
    weight_ref[...] = dot(sums_ref[...], jnp.concatenate([valid, valid], axis=0))


def remote_kernel(
    r0, r1, r2, r3, low_ref, high_ref, links_ref, part_ref, weight_ref, energy_ref,
    fold_ref, join_ref, fold_b_ref, join_b_ref,
    cond_ref, scaled_ref, b0, b1, b2, b3, lb, ub, rows_ref, *scratch,
):
    order_links(links_ref, rows_ref)
    chunks = []
    for ref in (r0, r1, r2, r3, low_ref, high_ref):
        for at in range(0, ref.shape[1], TILE):
            chunks.append(ref[:, at : at + TILE])
    total = gather_filtered(chunks, 4, rows_ref, fold_ref, join_ref, *scratch[:5])
    weight = weight_ref[...]
    filtered = (part_ref[...] + total) / weight
    square = filtered * filtered
    cond_ref[...] = floor_value + square * filtered * (1.0 - floor_value)
    scaled = -penalty * (1.0 - floor_value) * square * energy_ref[...] / weight
    scaled_ref[...] = scaled
    back = scatter_back(scaled, 4, len(chunks), rows_ref, fold_b_ref, join_b_ref, *scratch[5:])
    at = 0
    for ref in (b0, b1, b2, b3, lb, ub):
        for start in range(0, ref.shape[1], TILE):
            ref[:, start : start + TILE] = back[at]
            at += 1


def own_kernel(scaled_ref, links_ref, fold_b_ref, join_b_ref, own_ref, sens_ref, rows_ref, *scratch):
    order_links(links_ref, rows_ref)
    scaled = scaled_ref[...]
    heads = scaled.shape[1] // TILE
    back = scatter_back(scaled, 0, heads, rows_ref, fold_b_ref, join_b_ref, *scratch)
    sens_ref[...] = jnp.concatenate(back, axis=1) + dot(own_ref[...], pieces(scaled))


def final_kernel(live_ref, sens_ref, index_ref, face_ref, v0, v1, v2, v3, v4, v5, out_ref):
    heads = sens_ref.shape[1] // TILE
    groups = index_ref.shape[0]
    total = jnp.zeros((heads * 128, TILE), F32)
    for g, ref in enumerate((v0, v1, v2, v3, v4, v5)):
        if g < groups:
            idx = index_ref[g : g + 1, :]
            at = lax.broadcasted_iota(jnp.int32, idx.shape, 1)
            upper = jnp.where(at < live_ref[g], idx >> 8, -1)
        else:
            idx = face_ref[g - groups : g - groups + 1, :]
            upper = jnp.where(live_ref[g] > 0, idx >> 8, -1)
        hot = one_hot(idx & (TILE - 1))
        value = jnp.concatenate(split2(ref[...]), axis=0)
        parts = [value * (upper == h).astype(F32).astype(BF16) for h in range(heads)]
        total = total + dot_nt(jnp.concatenate(parts, axis=0), hot)
    for h in range(heads):
        cols = slice(h * TILE, h * TILE + TILE)
        both = total[h * 128 : h * 128 + 64] + total[h * 128 + 64 : h * 128 + 128]
        out_ref[:, cols] = sens_ref[:, cols] + both


def params():
    return pltpu.CompilerParams(vmem_limit_bytes=48 * 1024 * 1024)


def cost(us):
    return pl.CostEstimate(flops=int(us * 5e8), bytes_accessed=int(us * 2e6), transcendentals=0)


def gather_scratch(count, blocks):
    return [
        pltpu.VMEM((6, count * 32, 2 * TILE), BF16),
        pltpu.VMEM((12, count * 16, 2 * TILE), BF16),
        pltpu.VMEM((16, count * TILE), F32),
        pltpu.VMEM((6, 32, blocks), F32),
        pltpu.VMEM((12, 16, blocks), F32),
    ]


def scatter_scratch(count, blocks):
    return [
        pltpu.VMEM((6, 64, blocks), BF16),
        pltpu.VMEM((12, 32, blocks), BF16),
        pltpu.VMEM((8, 16, blocks), BF16),
        pltpu.VMEM((6, count * 32, TILE), F32),
        pltpu.VMEM((12, count * 16, TILE), F32),
        pltpu.VMEM((8, (count + 3) // 4 * 16, TILE), F32),
    ]


def passed_along(shard, axis, by):
    count = lax.axis_size(axis)
    pairs = [(i, (i + by) % count) for i in range(count)]
    return lax.ppermute(shard, axis, pairs)


def on_device(density, energy, links, send_index, send_live, face_index):
    const = {name: jnp.asarray(value) for name, value in constants().items()}
    blocks = density.shape[1]
    offsets = [offset for offset in range(-REACH, REACH + 1) if offset != 0]
    indices, faces_at = send_index[0, 0], face_index[0, 0]
    capacity, face_count = indices.shape[1], faces_at.shape[1]
    targets = jnp.concatenate(
        [lax.axis_index("plane") + np.array(offsets), lax.axis_index("depth") + np.array([-1, 1])]
    )
    ends = np.array([lax.axis_size("plane")] * len(offsets) + [lax.axis_size("depth")] * 2)
    counts = jnp.concatenate([send_live[0, 0], np.array([face_count] * 2, np.int32)])
    counts = jnp.where((targets >= 0) & (targets < ends), counts, 0)
    whole = jax.ShapeDtypeStruct((64, blocks), F32)
    listed = jax.ShapeDtypeStruct((64, capacity), F32)
    faced = jax.ShapeDtypeStruct((64, face_count), F32)
    vmem = pl.BlockSpec(memory_space=pltpu.VMEM)
    smem = pl.BlockSpec(memory_space=pltpu.SMEM)
    ordered = pltpu.VMEM((32, blocks), jnp.int32)

    loads = pl.pallas_call(
        payload_kernel,
        out_shape=[listed] * 4 + [faced] * 2,
        in_specs=[smem, vmem, vmem, vmem],
        out_specs=[vmem] * 6,
        compiler_params=params(),
        cost_estimate=cost(3),
    )(counts, density, indices, faces_at)
    received = [passed_along(loads[m], "plane", offset) for m, offset in enumerate(offsets)]
    from_low = passed_along(loads[5], "depth", 1)
    from_high = passed_along(loads[4], "depth", -1)
    part, weight = pl.pallas_call(
        local_kernel,
        out_shape=[whole, whole],
        in_specs=[vmem] * 6,
        out_specs=[vmem] * 2,
        scratch_shapes=[ordered] + gather_scratch(4, blocks),
        compiler_params=params(),
        cost_estimate=cost(8),
    )(density, links, const["fold_fwd"], const["join_fwd"], const["own"], const["sums"])
    conductivity, scaled, *groups_back = pl.pallas_call(
        remote_kernel,
        out_shape=[whole, whole] + [listed] * 4 + [faced] * 2,
        in_specs=[vmem] * 14,
        out_specs=[vmem] * 8,
        scratch_shapes=[ordered] + gather_scratch(10, blocks) + scatter_scratch(10, blocks),
        compiler_params=params(),
        cost_estimate=cost(20),
    )(
        *received, from_low, from_high, links, part, weight, energy,
        const["fold_fwd"], const["join_fwd"], const["fold_bwd"], const["join_bwd"],
    )
    returned = [passed_along(groups_back[m], "plane", -offset) for m, offset in enumerate(offsets)]
    to_one = passed_along(groups_back[4], "depth", -1)
    to_zero = passed_along(groups_back[5], "depth", 1)
    sens = pl.pallas_call(
        own_kernel,
        out_shape=whole,
        in_specs=[vmem] * 5,
        out_specs=vmem,
        scratch_shapes=[ordered] + scatter_scratch(4, blocks),
        compiler_params=params(),
        cost_estimate=cost(8),
    )(scaled, links, const["fold_bwd"], const["join_bwd"], const["own_t"])
    sens = pl.pallas_call(
        final_kernel,
        out_shape=whole,
        in_specs=[smem] + [vmem] * 9,
        out_specs=vmem,
        compiler_params=params(),
        cost_estimate=cost(3),
    )(counts, sens, indices, faces_at, *returned, to_zero, to_one)
    return (conductivity, sens)


def solution(mesh):
    in_specs = (
        P(None, ("plane", "depth")),
        P(None, ("plane", "depth")),
        P(None, ("plane", "depth")),
        P("plane", "depth", None, None),
        P("plane", "depth", None),
        P("plane", "depth", None, None),
    )
    out_specs = (P(None, ("plane", "depth")), P(None, ("plane", "depth")))
    return jax.shard_map(
        on_device, mesh=mesh, in_specs=in_specs, out_specs=out_specs, check_vma=False
    )
```

```python
import jax
import jax.numpy as jnp
import numpy as np
from jax import lax
from jax.experimental import pallas as pl
from jax.experimental.pallas import tpu as pltpu
from jax.sharding import PartitionSpec as P

REACH = 2
TILE = 256
OFFSETS = [offset for offset in range(-REACH, REACH + 1) if offset != 0]
OUTWARD = (2, 3, 1, 0)
BACKWARD = (0, 1, 2, 3)
LANE_LOCAL = 6
LANE_REMOTE = 2
radius = 3.0
floor_value = 0.001
penalty = 3.0

F32 = jnp.float32
BF16 = jnp.bfloat16

ORDERS = ((0, 1, 2), (2, 0, 1), (1, 2, 0))


def cone_table():
    voxels = np.arange(64)
    places = np.stack([voxels // 16, voxels // 4 % 4, voxels % 4], axis=-1)
    slots = np.arange(27)
    moved = np.stack([slots // 9 - 1, slots // 3 % 3 - 1, slots % 3 - 1], axis=-1) * 4
    apart = places[None, :, None, :] - places[None, None, :, :] - moved[:, None, None, :]
    squares = np.sum(apart * apart, axis=-1).astype(np.float32)
    return np.maximum(np.float32(0.0), np.float32(radius) - np.sqrt(squares))


def order_voxels(order):
    rows = np.arange(64)
    coords = np.zeros((3, 64), np.int64)
    coords[order[0]], coords[order[1]], coords[order[2]] = rows // 16, rows // 4 % 4, rows % 4
    return coords[0] * 16 + coords[1] * 4 + coords[2]


def slot_of(offset):
    return (offset[0] + 1) * 9 + (offset[1] + 1) * 3 + offset[2] + 1


def layout():
    faces, edges, corners = [], [], []
    for at, order in enumerate(ORDERS):
        for sign in (-1, 1):
            offset = [0, 0, 0]
            offset[order[0]] = sign
            faces.append((slot_of(offset), at, sign))
    for at, order in enumerate(ORDERS):
        for one in (-1, 1):
            for two in (-1, 1):
                offset = [0, 0, 0]
                offset[order[0]], offset[order[1]] = one, two
                edges.append((slot_of(offset), at, one, two))
    for a in (-1, 1):
        for b in (-1, 1):
            for c in (-1, 1):
                corners.append(slot_of((a, b, c)))
    return faces, edges, corners


FACES, EDGES, CORNERS = layout()
SLOTS = [f[0] for f in FACES] + [e[0] for e in EDGES] + CORNERS


def face_start(sign, forward):
    return 32 if (sign > 0) == forward else 0


def edge_starts(one, two, forward):
    first = 2 if (one > 0) == forward else 0
    second = 2 if (two > 0) == forward else 0
    return [(first + i) * 16 + second * 4 for i in range(2)]


def slot_rows(forward):
    voxels = [order_voxels(order) for order in ORDERS]
    out = []
    for slot, at, sign in FACES:
        start = face_start(sign, forward)
        out.append((slot, voxels[at][start : start + 32]))
    for slot, at, one, two in EDGES:
        rows = np.concatenate([voxels[at][s : s + 8] for s in edge_starts(one, two, forward)])
        out.append((slot, rows))
    return out


def pieces_np(table):
    high = table.astype(jnp.bfloat16)
    low = (table - high.astype(np.float32)).astype(jnp.bfloat16)
    return high, low


def three(table):
    high, low = pieces_np(table)
    return np.concatenate([high, low, high], axis=1)


def corner_rows(table, forward):
    out = []
    for slot in CORNERS:
        part = table[slot] if forward else table[slot].T
        counts = (part > 0).sum(axis=1)
        main = int(np.argmax(counts))
        rest = [int(v) for v in np.nonzero(counts)[0] if v != main]
        out.append((part, main, rest))
    return out


def constants():
    table = cone_table()
    fold_fwd = [table[slot][rows] for slot, rows in slot_rows(True)]
    fold_bwd = [table[slot].T[rows] for slot, rows in slot_rows(False)]
    cor_fwd, cor_bwd = corner_rows(table, True), corner_rows(table, False)
    fold_fwd += [np.stack([part[main] for part, main, rest in cor_fwd])]
    fold_fwd += [np.stack([part[rest[0]] for part, main, rest in cor_fwd])]
    for part, main, rest in cor_bwd:
        fold_bwd += [np.tile(np.stack([part[main], part[rest[0]]]), (8, 1))]
    spots = []
    for at in (1, 2):
        spot = np.zeros((64, 64), np.float32)
        spot[order_voxels(ORDERS[at]), np.arange(64)] = 1
        spots.append(spot)
    cf = np.zeros((64, 16), np.float32)
    for m, (part, main, rest) in enumerate(cor_fwd):
        cf[main, m] = 1
        cf[rest, 8 + m] = 1
    join_fwd = np.concatenate(spots + [cf], axis=1)
    join_fwd = np.concatenate([join_fwd, join_fwd], axis=1).astype(jnp.bfloat16)
    joins = []
    for parity in range(2):
        cb = np.zeros((64, 64), np.float32)
        for m, (part, main, rest) in enumerate(cor_bwd):
            for piece in range(2):
                cb[main, m * 8 + parity * 4 + piece * 2] = 1
                cb[rest, m * 8 + parity * 4 + piece * 2 + 1] = 1
        join = np.concatenate(spots + [cb], axis=1)
        joins.append(np.concatenate([join, join], axis=1))
    sums = table.sum(axis=2).T
    high, low = pieces_np(sums)
    return dict(
        fold_fwd=three(np.concatenate(fold_fwd)),
        fold_bwd=three(np.concatenate(fold_bwd)),
        own=three(table[13]),
        own_t=three(table[13].T),
        join_fwd=join_fwd,
        join_bwd=np.concatenate(joins).astype(jnp.bfloat16),
        sums=np.concatenate([high, low], axis=1),
    )


def split2(value):
    high = value.astype(BF16)
    return high, (value - high.astype(F32)).astype(BF16)


def pieces(value):
    high, low = split2(value)
    return jnp.concatenate([high, high, low], axis=0)


def dot(a, b):
    return jnp.dot(a, b, preferred_element_type=F32)


def dot_nt(a, b):
    return lax.dot_general(a, b, (((1,), (1,)), ((), ())), preferred_element_type=F32)


def one_hot(low):
    shape = (TILE, low.shape[1])
    low = low.astype(jnp.int16)
    hit = lax.broadcasted_iota(jnp.int16, shape, 0) == jnp.broadcast_to(low, shape)
    return jnp.where(hit, jnp.array(1, BF16), jnp.array(0, BF16))


def gather_filtered(chunks, ids, lane_edges, links_ref, fold_ref, join_ref, tf, te, yc):
    count = len(chunks)
    faces, edges = len(FACES), len(EDGES)
    blocks = links_ref.shape[1]
    cut = 192 + (edges - lane_edges) * 16
    for h, chunk in enumerate(chunks):
        y = dot(fold_ref[...], pieces(chunk))
        high, low = split2(y[:cut])
        for f in range(faces):
            tf[f, h * 32 : h * 32 + 32, 0:TILE] = high[f * 32 : f * 32 + 32]
            tf[f, h * 32 : h * 32 + 32, TILE : 2 * TILE] = low[f * 32 : f * 32 + 32]
        for e in range(edges - lane_edges):
            at = 192 + e * 16
            te[e, h * 16 : h * 16 + 16, 0:TILE] = high[at : at + 16]
            te[e, h * 16 : h * 16 + 16, TILE : 2 * TILE] = low[at : at + 16]
        yc[:, h * TILE : h * TILE + TILE] = y[cut:400]

    def by_matmul(slot, table, rows):
        out = []
        for nb in range(blocks // TILE):
            idx = links_ref[slot : slot + 1, nb * TILE : nb * TILE + TILE]
            hot = one_hot(idx & (TILE - 1))
            upper = jnp.broadcast_to(idx >> 8, (rows, TILE))
            got = dot(table[:, 0:TILE], hot) + dot(table[:, TILE : 2 * TILE], hot)
            acc = jnp.zeros((rows, TILE), F32)
            for h in range(count):
                acc = jnp.where(upper == ids[h], got[h * rows : h * rows + rows], acc)
            out.append(acc)
        return jnp.concatenate(out, axis=1)

    def by_lanes(index_of, at, groups):
        out = [[] for _ in range(groups)]
        for bg in range(blocks // 128):
            idx = index_of(slice(bg * 128, bg * 128 + 128))
            low, upper = idx & 127, idx >> 7
            acc = [jnp.zeros((8, 128), F32) for _ in range(groups)]
            for h in range(2 * count):
                hit = upper == 2 * ids[h // 2] + h % 2
                for c in range(groups):
                    rows = slice(at + c * 8, at + c * 8 + 8)
                    got = jnp.take_along_axis(yc[rows, h * 128 : h * 128 + 128], low, axis=1)
                    acc[c] = jnp.where(hit, got, acc[c])
            for c in range(groups):
                out[c].append(acc[c])
        return jnp.concatenate([jnp.concatenate(c, axis=1) for c in out], axis=0)

    def edge_lanes(e):
        slot = EDGES[e][0]
        at = (e - edges + lane_edges) * 16
        return by_lanes(
            lambda cols: jnp.broadcast_to(links_ref[slot : slot + 1, cols], (8, 128)), at, 2
        )

    def corner_index(cols):
        return jnp.concatenate([links_ref[slot : slot + 1, cols] for slot in CORNERS], axis=0)

    lanes = [(edge_lanes, e) for e in range(edges - lane_edges, edges)]
    lanes.append((lambda _: by_lanes(corner_index, lane_edges * 16, 2), "corner"))
    matmuls = [(FACES[f][0], tf.at[f], 32, f) for f in range(faces)]
    matmuls += [(EDGES[e][0], te.at[e], 16, faces + e) for e in range(edges - lane_edges)]
    found = {}
    done = 0
    for i, (slot, table, rows, name) in enumerate(matmuls):
        found[name] = by_matmul(slot, table, rows)
        while done < len(lanes) and done * len(matmuls) <= i * len(lanes):
            fn, e = lanes[done]
            found[e if e == "corner" else faces + e] = fn(e)
            done += 1
    for fn, e in lanes[done:]:
        found[e if e == "corner" else faces + e] = fn(e)
    totals = order_totals(lambda f: found[f], lambda e: found[faces + e], True)
    high, low = split2(jnp.concatenate([totals[1], totals[2], found["corner"]], axis=0))
    return totals[0] + dot(join_ref[...], jnp.concatenate([high, low], axis=0))


def order_totals(face, edge, forward):
    totals = []
    for at in range(3):
        runs = [None] * 8
        for f, (_, order, sign) in enumerate(FACES):
            if order == at:
                value, start = face(f), face_start(sign, forward)
                for i in range(4):
                    runs[start // 8 + i] = value[i * 8 : i * 8 + 8]
        for e, (_, order, one, two) in enumerate(EDGES):
            if order == at:
                value = edge(e)
                for i, start in enumerate(edge_starts(one, two, forward)):
                    runs[start // 8] = runs[start // 8] + value[i * 8 : i * 8 + 8]
        totals.append(jnp.concatenate(runs, axis=0))
    return totals


def scatter_back(scaled, ids, links_ref, fold_ref, join_ref):
    count = len(ids)
    blocks = links_ref.shape[1]
    spread = dot(fold_ref[...], pieces(scaled))

    quarter = lax.broadcasted_iota(jnp.int32, (16, blocks), 0) // 4
    quarters = []
    for q in range((count + 3) // 4):
        rows_for = jnp.full((16, blocks), -1, jnp.int32)
        for i, h in enumerate(ids[4 * q : 4 * q + 4]):
            rows_for = jnp.where(quarter == i, h, rows_for)
        quarters.append(rows_for)

    def one_slot(slot, value, rows):
        idx = links_ref[slot : slot + 1, :]
        hot = one_hot(idx & (TILE - 1))
        upper = idx >> 8
        parts = [value * (upper == h).astype(F32).astype(BF16) for h in ids]
        got = dot_nt(jnp.concatenate(parts, axis=0), hot)
        return [
            got[h * 2 * rows : h * 2 * rows + rows] + got[h * 2 * rows + rows : h * 2 * rows + 2 * rows]
            for h in range(count)
        ]

    def one_corner(m):
        idx = links_ref[CORNERS[m] : CORNERS[m] + 1, :]
        hot = one_hot(idx & (TILE - 1))
        upper = jnp.broadcast_to(idx >> 8, (16, blocks))
        is_high = lax.broadcasted_iota(jnp.int32, (16, blocks), 0) % 4 < 2
        part = spread[384 + m * 16 : 384 + m * 16 + 16]
        top = part.astype(BF16).astype(F32)
        value = jnp.where(is_high, top, part - top).astype(BF16)
        parts = [
            value * (upper == quarters[q]).astype(F32).astype(BF16) for q in range(len(quarters))
        ]
        return dot_nt(jnp.concatenate(parts, axis=0), hot)

    def both(at, rows):
        return jnp.concatenate(split2(spread[at : at + rows]), axis=0)

    faces = [one_slot(face[0], both(f * 32, 32), 32) for f, face in enumerate(FACES)]
    edges = [one_slot(edge[0], both(192 + e * 16, 16), 16) for e, edge in enumerate(EDGES)]
    corners = [one_corner(m) for m in range(len(CORNERS))]
    out = []
    for h in range(count):
        totals = order_totals(lambda f: faces[f][h], lambda e: edges[e][h], False)
        tops = [corner[h // 2 * 8 : h // 2 * 8 + 8] for corner in corners]
        high, low = split2(jnp.concatenate([totals[1], totals[2]] + tops, axis=0))
        join = join_ref[h % 2 * 64 : h % 2 * 64 + 64, :]
        out.append(totals[0] + dot(join, jnp.concatenate([high, low], axis=0)))
    return out


def chunk_ids(order, heads):
    out = []
    for g in order:
        out += [heads + 2 * g, heads + 2 * g + 1]
    return out + [heads + 8, heads + 9]


def list_uppers(order, live_ref, index_ref, face_ref):
    place, places = lax.axis_index("plane"), lax.axis_size("plane")
    level, levels = lax.axis_index("depth"), lax.axis_size("depth")
    out = []
    for g in order:
        offset = OFFSETS[g]
        idx = index_ref[0, 0, g : g + 1, :]
        target = place + offset
        live = jnp.where((target >= 0) & (target < places), live_ref[0, 0, g], 0)
        at = lax.broadcasted_iota(jnp.int32, idx.shape, 1)
        out.append((idx, jnp.where(at < live, idx >> 8, -1)))
    for side, by in enumerate((-1, 1)):
        idx = face_ref[0, 0, side : side + 1, :]
        target = level + by
        live = jnp.where((target >= 0) & (target < levels), idx.shape[1], 0)
        at = lax.broadcasted_iota(jnp.int32, idx.shape, 1)
        out.append((idx, jnp.where(at < live, idx >> 8, -1)))
    return out


def payload_kernel(live_hbm, density_hbm, index_hbm, face_hbm, *refs):
    outs = refs[:6]
    live_ref, density_ref, index_ref, face_ref, sems = refs[6:]
    copies = [
        pltpu.make_async_copy(source, target, sems.at[at])
        for at, (source, target) in enumerate(
            [(density_hbm, density_ref), (live_hbm, live_ref), (index_hbm, index_ref), (face_hbm, face_ref)]
        )
    ]
    for copy in copies:
        copy.start()
    for copy in copies:
        copy.wait()
    density = density_ref[...]
    high, low = split2(density)
    heads = density.shape[1] // TILE
    table = jnp.concatenate(
        [
            jnp.concatenate([p[:, h * TILE : h * TILE + TILE] for h in range(heads)], axis=0)
            for p in (high, low)
        ],
        axis=1,
    )
    for ref, (idx, upper) in zip(outs, list_uppers(OUTWARD, live_ref, index_ref, face_ref)):
        hot = one_hot(idx & (TILE - 1))
        got = dot(table[:, 0:TILE], hot) + dot(table[:, TILE : 2 * TILE], hot)
        upper = jnp.broadcast_to(upper, (64, idx.shape[1]))
        acc = jnp.zeros((64, idx.shape[1]), F32)
        for h in range(heads):
            acc = jnp.where(upper == h, got[h * 64 : h * 64 + 64], acc)
        ref[...] = acc


def local_kernel(
    density_ref, links_ref, fold_ref, join_ref, own_ref, sums_ref, part_ref, weight_ref, *scratch
):
    density = density_ref[...]
    heads = density.shape[1] // TILE
    chunks = [density[:, h * TILE : h * TILE + TILE] for h in range(heads)]
    part = gather_filtered(chunks, list(range(heads)), LANE_LOCAL, links_ref, fold_ref, join_ref, *scratch)
    part_ref[...] = part + dot(own_ref[...], pieces(density))
    valid = (links_ref[...] != 14 * TILE).astype(F32).astype(BF16)
    weight_ref[...] = dot(sums_ref[...], jnp.concatenate([valid, valid], axis=0))


def remote_kernel(
    r0, r1, r2, r3, low_ref, high_ref, links_ref, part_ref, weight_ref, energy_ref,
    fold_ref, join_ref, fold_b_ref, join_b_ref,
    cond_ref, scaled_ref, b0, b1, b2, b3, lb, ub, *scratch,
):
    heads = part_ref.shape[1] // TILE
    chunks = []
    for ref in (r0, r1, r2, r3, low_ref, high_ref):
        for at in range(0, ref.shape[1], TILE):
            chunks.append(ref[:, at : at + TILE])
    total = gather_filtered(chunks, chunk_ids(OUTWARD, heads), LANE_REMOTE, links_ref, fold_ref, join_ref, *scratch)
    weight = weight_ref[...]
    filtered = (part_ref[...] + total) / weight
    square = filtered * filtered
    cond_ref[...] = floor_value + square * filtered * (1.0 - floor_value)
    scaled = -penalty * (1.0 - floor_value) * square * energy_ref[...] / weight
    scaled_ref[...] = scaled
    back = scatter_back(scaled, chunk_ids(BACKWARD, heads), links_ref, fold_b_ref, join_b_ref)
    at = 0
    for ref in (b0, b1, b2, b3, lb, ub):
        for start in range(0, ref.shape[1], TILE):
            ref[:, start : start + TILE] = back[at]
            at += 1


def own_kernel(scaled_ref, links_ref, fold_b_ref, join_b_ref, own_ref, sens_ref):
    scaled = scaled_ref[...]
    heads = scaled.shape[1] // TILE
    back = scatter_back(scaled, list(range(heads)), links_ref, fold_b_ref, join_b_ref)
    sens_ref[...] = jnp.concatenate(back, axis=1) + dot(own_ref[...], pieces(scaled))


def final_kernel(live_ref, sens_ref, index_ref, face_ref, v0, v1, v2, v3, v4, v5, out_ref):
    heads = sens_ref.shape[1] // TILE
    total = jnp.zeros((heads * 128, TILE), F32)
    lists = list_uppers(BACKWARD, live_ref, index_ref, face_ref)
    for ref, (idx, upper) in zip((v0, v1, v2, v3, v4, v5), lists):
        hot = one_hot(idx & (TILE - 1))
        value = jnp.concatenate(split2(ref[...]), axis=0)
        parts = [value * (upper == h).astype(F32).astype(BF16) for h in range(heads)]
        total = total + dot_nt(jnp.concatenate(parts, axis=0), hot)
    for h in range(heads):
        cols = slice(h * TILE, h * TILE + TILE)
        both = total[h * 128 : h * 128 + 64] + total[h * 128 + 64 : h * 128 + 128]
        out_ref[:, cols] = sens_ref[:, cols] + both


def params():
    return pltpu.CompilerParams(vmem_limit_bytes=48 * 1024 * 1024)


def cost(us):
    return pl.CostEstimate(flops=int(us * 5e8), bytes_accessed=int(us * 2e6), transcendentals=0)


def gather_scratch(count, lane_edges):
    return [
        pltpu.VMEM((6, count * 32, 2 * TILE), BF16),
        pltpu.VMEM((12 - lane_edges, count * 16, 2 * TILE), BF16),
        pltpu.VMEM((16 + lane_edges * 16, count * TILE), F32),
    ]


def passed_along(shard, axis, by):
    count = lax.axis_size(axis)
    pairs = [(i, (i + by) % count) for i in range(count)]
    return lax.ppermute(shard, axis, pairs)


def on_device(density, energy, links, send_index, send_live, face_index):
    const = {name: jnp.asarray(value) for name, value in constants().items()}
    blocks = density.shape[1]
    capacity, face_count = send_index.shape[3], face_index.shape[3]
    whole = jax.ShapeDtypeStruct((64, blocks), F32)
    listed = jax.ShapeDtypeStruct((64, capacity), F32)
    faced = jax.ShapeDtypeStruct((64, face_count), F32)
    vmem = pl.BlockSpec(memory_space=pltpu.VMEM)
    smem = pl.BlockSpec(memory_space=pltpu.SMEM)

    loads = pl.pallas_call(
        payload_kernel,
        out_shape=[listed] * 4 + [faced] * 2,
        in_specs=[pl.BlockSpec(memory_space=pl.ANY)] * 4,
        out_specs=[vmem] * 6,
        scratch_shapes=[
            pltpu.SMEM(send_live.shape, jnp.int32),
            pltpu.VMEM(density.shape, F32),
            pltpu.VMEM(send_index.shape, jnp.int32),
            pltpu.VMEM(face_index.shape, jnp.int32),
            pltpu.SemaphoreType.DMA((4,)),
        ],
        compiler_params=pltpu.CompilerParams(vmem_limit_bytes=63 * 1024 * 1024),
        cost_estimate=cost(3),
    )(send_live, density, send_index, face_index)
    received = [passed_along(loads[at], "plane", OFFSETS[g]) for at, g in enumerate(OUTWARD)]
    from_low = passed_along(loads[5], "depth", 1)
    from_high = passed_along(loads[4], "depth", -1)
    part, weight = pl.pallas_call(
        local_kernel,
        out_shape=[whole, whole],
        in_specs=[vmem] * 6,
        out_specs=[vmem] * 2,
        scratch_shapes=gather_scratch(4, LANE_LOCAL),
        compiler_params=params(),
        cost_estimate=cost(8),
    )(density, links, const["fold_fwd"], const["join_fwd"], const["own"], const["sums"])
    conductivity, scaled, *groups_back = pl.pallas_call(
        remote_kernel,
        out_shape=[whole, whole] + [listed] * 4 + [faced] * 2,
        in_specs=[vmem] * 14,
        out_specs=[vmem] * 8,
        scratch_shapes=gather_scratch(10, LANE_REMOTE),
        compiler_params=params(),
        cost_estimate=cost(20),
    )(
        *received, from_low, from_high, links, part, weight, energy,
        const["fold_fwd"], const["join_fwd"], const["fold_bwd"], const["join_bwd"],
    )
    returned = [passed_along(groups_back[at], "plane", -OFFSETS[g]) for at, g in enumerate(BACKWARD)]
    to_one = passed_along(groups_back[4], "depth", -1)
    to_zero = passed_along(groups_back[5], "depth", 1)
    sens = pl.pallas_call(
        own_kernel,
        out_shape=whole,
        in_specs=[vmem] * 5,
        out_specs=vmem,
        compiler_params=params(),
        cost_estimate=cost(8),
    )(scaled, links, const["fold_bwd"], const["join_bwd"], const["own_t"])
    sens = pl.pallas_call(
        final_kernel,
        out_shape=whole,
        in_specs=[smem] + [vmem] * 9,
        out_specs=vmem,
        compiler_params=params(),
        cost_estimate=cost(3),
    )(send_live, sens, send_index, face_index, *returned, to_zero, to_one)
    return (conductivity, sens)


def solution(mesh):
    in_specs = (
        P(None, ("plane", "depth")),
        P(None, ("plane", "depth")),
        P(None, ("plane", "depth")),
        P("plane", "depth", None, None),
        P("plane", "depth", None),
        P("plane", "depth", None, None),
    )
    out_specs = (P(None, ("plane", "depth")), P(None, ("plane", "depth")))
    return jax.shard_map(
        on_device, mesh=mesh, in_specs=in_specs, out_specs=out_specs, check_vma=False
    )
```

```python
import jax
import jax.numpy as jnp
import numpy as np
from jax import lax
from jax.experimental import pallas as pl
from jax.experimental.pallas import tpu as pltpu
from jax.sharding import PartitionSpec as P

REACH = 2
TILE = 256
OFFSETS = [offset for offset in range(-REACH, REACH + 1) if offset != 0]
OUTWARD = (2, 3, 1, 0)
BACKWARD = (0, 1, 2, 3)
LANE_LOCAL = 6
LANE_EARLY = 5
LANE_REMOTE = 6
radius = 3.0
floor_value = 0.001
penalty = 3.0

F32 = jnp.float32
BF16 = jnp.bfloat16

ORDERS = ((0, 1, 2), (2, 0, 1), (1, 2, 0))


def cone_table():
    voxels = np.arange(64)
    places = np.stack([voxels // 16, voxels // 4 % 4, voxels % 4], axis=-1)
    slots = np.arange(27)
    moved = np.stack([slots // 9 - 1, slots // 3 % 3 - 1, slots % 3 - 1], axis=-1) * 4
    apart = places[None, :, None, :] - places[None, None, :, :] - moved[:, None, None, :]
    squares = np.sum(apart * apart, axis=-1).astype(np.float32)
    return np.maximum(np.float32(0.0), np.float32(radius) - np.sqrt(squares))


def order_voxels(order):
    rows = np.arange(64)
    coords = np.zeros((3, 64), np.int64)
    coords[order[0]], coords[order[1]], coords[order[2]] = rows // 16, rows // 4 % 4, rows % 4
    return coords[0] * 16 + coords[1] * 4 + coords[2]


def slot_of(offset):
    return (offset[0] + 1) * 9 + (offset[1] + 1) * 3 + offset[2] + 1


def layout():
    faces, edges, corners = [], [], []
    for at, order in enumerate(ORDERS):
        for sign in (-1, 1):
            offset = [0, 0, 0]
            offset[order[0]] = sign
            faces.append((slot_of(offset), at, sign))
    for at, order in enumerate(ORDERS):
        for one in (-1, 1):
            for two in (-1, 1):
                offset = [0, 0, 0]
                offset[order[0]], offset[order[1]] = one, two
                edges.append((slot_of(offset), at, one, two))
    for a in (-1, 1):
        for b in (-1, 1):
            for c in (-1, 1):
                corners.append(slot_of((a, b, c)))
    return faces, edges, corners


FACES, EDGES, CORNERS = layout()
SLOTS = [f[0] for f in FACES] + [e[0] for e in EDGES] + CORNERS


def face_start(sign, forward):
    return 32 if (sign > 0) == forward else 0


def edge_starts(one, two, forward):
    first = 2 if (one > 0) == forward else 0
    second = 2 if (two > 0) == forward else 0
    return [(first + i) * 16 + second * 4 for i in range(2)]


def slot_rows(forward):
    voxels = [order_voxels(order) for order in ORDERS]
    out = []
    for slot, at, sign in FACES:
        start = face_start(sign, forward)
        out.append((slot, voxels[at][start : start + 32]))
    for slot, at, one, two in EDGES:
        rows = np.concatenate([voxels[at][s : s + 8] for s in edge_starts(one, two, forward)])
        out.append((slot, rows))
    return out


def pieces_np(table):
    high = table.astype(jnp.bfloat16)
    low = (table - high.astype(np.float32)).astype(jnp.bfloat16)
    return high, low


def three(table):
    high, low = pieces_np(table)
    return np.concatenate([high, low, high], axis=1)


def corner_rows(table, forward):
    out = []
    for slot in CORNERS:
        part = table[slot] if forward else table[slot].T
        counts = (part > 0).sum(axis=1)
        main = int(np.argmax(counts))
        rest = [int(v) for v in np.nonzero(counts)[0] if v != main]
        out.append((part, main, rest))
    return out


def constants():
    table = cone_table()
    fold_fwd = [table[slot][rows] for slot, rows in slot_rows(True)]
    fold_bwd = [table[slot].T[rows] for slot, rows in slot_rows(False)]
    cor_fwd, cor_bwd = corner_rows(table, True), corner_rows(table, False)
    fold_fwd += [np.stack([part[main] for part, main, rest in cor_fwd])]
    fold_fwd += [np.stack([part[rest[0]] for part, main, rest in cor_fwd])]
    for part, main, rest in cor_bwd:
        fold_bwd += [np.tile(np.stack([part[main], part[rest[0]]]), (8, 1))]
    spots = []
    for at in (1, 2):
        spot = np.zeros((64, 64), np.float32)
        spot[order_voxels(ORDERS[at]), np.arange(64)] = 1
        spots.append(spot)
    cf = np.zeros((64, 16), np.float32)
    for m, (part, main, rest) in enumerate(cor_fwd):
        cf[main, m] = 1
        cf[rest, 8 + m] = 1
    join_fwd = np.concatenate(spots + [cf], axis=1)
    join_fwd = np.concatenate([join_fwd, join_fwd], axis=1).astype(jnp.bfloat16)
    joins = []
    for parity in range(2):
        cb = np.zeros((64, 64), np.float32)
        for m, (part, main, rest) in enumerate(cor_bwd):
            for piece in range(2):
                cb[main, m * 8 + parity * 4 + piece * 2] = 1
                cb[rest, m * 8 + parity * 4 + piece * 2 + 1] = 1
        join = np.concatenate(spots + [cb], axis=1)
        joins.append(np.concatenate([join, join], axis=1))
    sums = table.sum(axis=2).T
    high, low = pieces_np(sums)
    return dict(
        fold_fwd=three(np.concatenate(fold_fwd)),
        fold_bwd=three(np.concatenate(fold_bwd)),
        own=three(table[13]),
        own_t=three(table[13].T),
        join_fwd=join_fwd,
        join_bwd=np.concatenate(joins).astype(jnp.bfloat16),
        sums=np.concatenate([high, low], axis=1),
    )


def split2(value):
    high = value.astype(BF16)
    return high, (value - high.astype(F32)).astype(BF16)


def pieces(value):
    high, low = split2(value)
    return jnp.concatenate([high, high, low], axis=0)


def dot(a, b):
    return jnp.dot(a, b, preferred_element_type=F32)


def dot_nt(a, b):
    return lax.dot_general(a, b, (((1,), (1,)), ((), ())), preferred_element_type=F32)


def one_hot(low):
    shape = (TILE, low.shape[1])
    low = low.astype(jnp.int16)
    hit = lax.broadcasted_iota(jnp.int16, shape, 0) == jnp.broadcast_to(low, shape)
    return jnp.where(hit, jnp.array(1, BF16), jnp.array(0, BF16))


def gather_filtered(chunks, ids, lane_edges, links_ref, fold_ref, join_ref, tf, te, yc):
    count = len(chunks)
    faces, edges = len(FACES), len(EDGES)
    blocks = links_ref.shape[1]
    cut = 192 + (edges - lane_edges) * 16
    for h, chunk in enumerate(chunks):
        y = dot(fold_ref[...], pieces(chunk))
        high, low = split2(y[:cut])
        for f in range(faces):
            tf[f, h * 32 : h * 32 + 32, 0:TILE] = high[f * 32 : f * 32 + 32]
            tf[f, h * 32 : h * 32 + 32, TILE : 2 * TILE] = low[f * 32 : f * 32 + 32]
        for e in range(edges - lane_edges):
            at = 192 + e * 16
            te[e, h * 16 : h * 16 + 16, 0:TILE] = high[at : at + 16]
            te[e, h * 16 : h * 16 + 16, TILE : 2 * TILE] = low[at : at + 16]
        yc[:, h * TILE : h * TILE + TILE] = y[cut:400]

    def by_matmul(slot, table, rows):
        out = []
        for nb in range(blocks // TILE):
            idx = links_ref[slot : slot + 1, nb * TILE : nb * TILE + TILE]
            hot = one_hot(idx & (TILE - 1))
            upper = jnp.broadcast_to(idx >> 8, (rows, TILE))
            got = dot(table[:, 0:TILE], hot) + dot(table[:, TILE : 2 * TILE], hot)
            acc = jnp.zeros((rows, TILE), F32)
            for h in range(count):
                acc = jnp.where(upper == ids[h], got[h * rows : h * rows + rows], acc)
            out.append(acc)
        return jnp.concatenate(out, axis=1)

    def by_lanes(index_of, at, groups):
        out = [[] for _ in range(groups)]
        for bg in range(blocks // 128):
            idx = index_of(slice(bg * 128, bg * 128 + 128))
            low, upper = idx & 127, idx >> 7
            acc = [jnp.zeros((8, 128), F32) for _ in range(groups)]
            for h in range(2 * count):
                hit = upper == 2 * ids[h // 2] + h % 2
                for c in range(groups):
                    rows = slice(at + c * 8, at + c * 8 + 8)
                    got = jnp.take_along_axis(yc[rows, h * 128 : h * 128 + 128], low, axis=1)
                    acc[c] = jnp.where(hit, got, acc[c])
            for c in range(groups):
                out[c].append(acc[c])
        return jnp.concatenate([jnp.concatenate(c, axis=1) for c in out], axis=0)

    def edge_lanes(e):
        slot = EDGES[e][0]
        at = (e - edges + lane_edges) * 16
        return by_lanes(
            lambda cols: jnp.broadcast_to(links_ref[slot : slot + 1, cols], (8, 128)), at, 2
        )

    def corner_index(cols):
        return jnp.concatenate([links_ref[slot : slot + 1, cols] for slot in CORNERS], axis=0)

    lanes = [(edge_lanes, e) for e in range(edges - lane_edges, edges)]
    lanes.append((lambda _: by_lanes(corner_index, lane_edges * 16, 2), "corner"))
    matmuls = [(FACES[f][0], tf.at[f], 32, f) for f in range(faces)]
    matmuls += [(EDGES[e][0], te.at[e], 16, faces + e) for e in range(edges - lane_edges)]
    found = {}
    done = 0
    for i, (slot, table, rows, name) in enumerate(matmuls):
        found[name] = by_matmul(slot, table, rows)
        while done < len(lanes) and done * len(matmuls) <= i * len(lanes):
            fn, e = lanes[done]
            found[e if e == "corner" else faces + e] = fn(e)
            done += 1
    for fn, e in lanes[done:]:
        found[e if e == "corner" else faces + e] = fn(e)
    totals = order_totals(lambda f: found[f], lambda e: found[faces + e], True)
    high, low = split2(jnp.concatenate([totals[1], totals[2], found["corner"]], axis=0))
    return totals[0] + dot(join_ref[...], jnp.concatenate([high, low], axis=0))


def order_totals(face, edge, forward):
    totals = []
    for at in range(3):
        runs = [None] * 8
        for f, (_, order, sign) in enumerate(FACES):
            if order == at:
                value, start = face(f), face_start(sign, forward)
                for i in range(4):
                    runs[start // 8 + i] = value[i * 8 : i * 8 + 8]
        for e, (_, order, one, two) in enumerate(EDGES):
            if order == at:
                value = edge(e)
                for i, start in enumerate(edge_starts(one, two, forward)):
                    runs[start // 8] = runs[start // 8] + value[i * 8 : i * 8 + 8]
        totals.append(jnp.concatenate(runs, axis=0))
    return totals


def scatter_back(scaled, ids, kind, links_ref, fold_ref, join_ref):
    count = len(ids)
    blocks = links_ref.shape[1]
    spread = dot(fold_ref[...], pieces(scaled))
    lows = jnp.transpose((links_ref[...] & (TILE - 1)).astype(F32))
    lane = lax.broadcasted_iota(jnp.int32, (blocks, TILE), 1).astype(F32).astype(kind)

    def hot_rows(slot):
        low = jnp.broadcast_to(lows[:, slot : slot + 1], (blocks, TILE)).astype(kind)
        return jnp.where(lane == low, jnp.array(1, kind), jnp.array(0, kind)).astype(BF16)


    quarter = lax.broadcasted_iota(jnp.int32, (16, blocks), 0) // 4
    quarters = []
    for q in range((count + 3) // 4):
        rows_for = jnp.full((16, blocks), -1, jnp.int32)
        for i, h in enumerate(ids[4 * q : 4 * q + 4]):
            rows_for = jnp.where(quarter == i, h, rows_for)
        quarters.append(rows_for)

    def one_slot(slot, value, rows):
        idx = links_ref[slot : slot + 1, :]
        hot = hot_rows(slot)
        upper = idx >> 8
        parts = [value * (upper == h).astype(F32).astype(BF16) for h in ids]
        got = dot(jnp.concatenate(parts, axis=0), hot)
        return [
            got[h * 2 * rows : h * 2 * rows + rows] + got[h * 2 * rows + rows : h * 2 * rows + 2 * rows]
            for h in range(count)
        ]

    def one_corner(m):
        idx = links_ref[CORNERS[m] : CORNERS[m] + 1, :]
        hot = hot_rows(CORNERS[m])
        upper = jnp.broadcast_to(idx >> 8, (16, blocks))
        is_high = lax.broadcasted_iota(jnp.int32, (16, blocks), 0) % 4 < 2
        part = spread[384 + m * 16 : 384 + m * 16 + 16]
        top = part.astype(BF16).astype(F32)
        value = jnp.where(is_high, top, part - top).astype(BF16)
        parts = [
            value * (upper == quarters[q]).astype(F32).astype(BF16) for q in range(len(quarters))
        ]
        return dot(jnp.concatenate(parts, axis=0), hot)

    def both(at, rows):
        return jnp.concatenate(split2(spread[at : at + rows]), axis=0)

    faces = [one_slot(face[0], both(f * 32, 32), 32) for f, face in enumerate(FACES)]
    edges = [one_slot(edge[0], both(192 + e * 16, 16), 16) for e, edge in enumerate(EDGES)]
    corners = [one_corner(m) for m in range(len(CORNERS))]
    out = []
    for h in range(count):
        totals = order_totals(lambda f: faces[f][h], lambda e: edges[e][h], False)
        tops = [corner[h // 2 * 8 : h // 2 * 8 + 8] for corner in corners]
        high, low = split2(jnp.concatenate([totals[1], totals[2]] + tops, axis=0))
        join = join_ref[h % 2 * 64 : h % 2 * 64 + 64, :]
        out.append(totals[0] + dot(join, jnp.concatenate([high, low], axis=0)))
    return out


def chunk_ids(order, heads):
    out = []
    for g in order:
        out += [heads + 2 * g, heads + 2 * g + 1]
    return out + [heads + 8, heads + 9]


def list_uppers(order, live_ref, index_ref, face_ref):
    place, places = lax.axis_index("plane"), lax.axis_size("plane")
    level, levels = lax.axis_index("depth"), lax.axis_size("depth")
    out = []
    for g in order:
        offset = OFFSETS[g]
        idx = index_ref[0, 0, g : g + 1, :]
        target = place + offset
        live = jnp.where((target >= 0) & (target < places), live_ref[0, 0, g], 0)
        at = lax.broadcasted_iota(jnp.int32, idx.shape, 1)
        out.append((idx, jnp.where(at < live, idx >> 8, -1)))
    for side, by in enumerate((-1, 1)):
        idx = face_ref[0, 0, side : side + 1, :]
        target = level + by
        live = jnp.where((target >= 0) & (target < levels), idx.shape[1], 0)
        at = lax.broadcasted_iota(jnp.int32, idx.shape, 1)
        out.append((idx, jnp.where(at < live, idx >> 8, -1)))
    return out


def payload_kernel(live_hbm, density_hbm, index_hbm, face_hbm, *refs):
    outs = refs[:6]
    live_ref, density_ref, index_ref, face_ref, sems = refs[6:]
    copies = [
        pltpu.make_async_copy(source, target, sems.at[at])
        for at, (source, target) in enumerate(
            [(density_hbm, density_ref), (live_hbm, live_ref), (index_hbm, index_ref), (face_hbm, face_ref)]
        )
    ]
    for copy in copies:
        copy.start()
    for copy in copies:
        copy.wait()
    density = density_ref[...]
    high, low = split2(density)
    heads = density.shape[1] // TILE
    table = jnp.concatenate(
        [
            jnp.concatenate([p[:, h * TILE : h * TILE + TILE] for h in range(heads)], axis=0)
            for p in (high, low)
        ],
        axis=1,
    )
    for ref, (idx, upper) in zip(outs, list_uppers(OUTWARD, live_ref, index_ref, face_ref)):
        hot = one_hot(idx & (TILE - 1))
        got = dot(table[:, 0:TILE], hot) + dot(table[:, TILE : 2 * TILE], hot)
        upper = jnp.broadcast_to(upper, (64, idx.shape[1]))
        acc = jnp.zeros((64, idx.shape[1]), F32)
        for h in range(heads):
            acc = jnp.where(upper == h, got[h * 64 : h * 64 + 64], acc)
        ref[...] = acc


def local_kernel(
    density_ref, links_ref, fold_ref, join_ref, own_ref, sums_ref, part_ref, weight_ref, *scratch
):
    density = density_ref[...]
    heads = density.shape[1] // TILE
    chunks = [density[:, h * TILE : h * TILE + TILE] for h in range(heads)]
    part = gather_filtered(chunks, list(range(heads)), LANE_LOCAL, links_ref, fold_ref, join_ref, *scratch)
    part_ref[...] = part + dot(own_ref[...], pieces(density))
    valid = (links_ref[...] != 14 * TILE).astype(F32).astype(BF16)
    weight_ref[...] = dot(sums_ref[...], jnp.concatenate([valid, valid], axis=0))


def tile_chunks(refs):
    return [ref[:, at : at + TILE] for ref in refs for at in range(0, ref.shape[1], TILE)]


def early_kernel(r0, r1, low_ref, high_ref, links_ref, part_ref, fold_ref, join_ref, out_ref, *scratch):
    ids = chunk_ids(OUTWARD, part_ref.shape[1] // TILE)
    chunks = tile_chunks((r0, r1, low_ref, high_ref))
    total = gather_filtered(chunks, ids[:4] + ids[8:], LANE_EARLY, links_ref, fold_ref, join_ref, *scratch)
    out_ref[...] = part_ref[...] + total


def remote_kernel(
    r0, r1, r2, r3, links_ref, part_ref, weight_ref, energy_ref,
    fold_ref, join_ref, fold_b_ref, join_b_ref,
    cond_ref, scaled_ref, b0, b1, b2, b3, lb, ub, *scratch,
):
    heads = part_ref.shape[1] // TILE
    chunks = tile_chunks((r2, r3))
    total = gather_filtered(chunks, chunk_ids(OUTWARD, heads)[4:8], LANE_REMOTE, links_ref, fold_ref, join_ref, *scratch)
    weight = weight_ref[...]
    filtered = (part_ref[...] + total) / weight
    square = filtered * filtered
    cond_ref[...] = floor_value + square * filtered * (1.0 - floor_value)
    scaled = -penalty * (1.0 - floor_value) * square * energy_ref[...] / weight
    scaled_ref[...] = scaled
    back = scatter_back(scaled, chunk_ids(BACKWARD, heads), F32, links_ref, fold_b_ref, join_b_ref)
    at = 0
    for ref in (b0, b1, b2, b3, lb, ub):
        for start in range(0, ref.shape[1], TILE):
            ref[:, start : start + TILE] = back[at]
            at += 1


def own_kernel(scaled_ref, links_ref, fold_b_ref, join_b_ref, own_ref, sens_ref):
    scaled = scaled_ref[...]
    heads = scaled.shape[1] // TILE
    back = scatter_back(scaled, list(range(heads)), BF16, links_ref, fold_b_ref, join_b_ref)
    sens_ref[...] = jnp.concatenate(back, axis=1) + dot(own_ref[...], pieces(scaled))


def final_kernel(live_ref, sens_ref, index_ref, face_ref, v0, v1, v2, v3, v4, v5, out_ref):
    heads = sens_ref.shape[1] // TILE
    total = jnp.zeros((heads * 128, TILE), F32)
    lists = list_uppers(BACKWARD, live_ref, index_ref, face_ref)
    for ref, (idx, upper) in zip((v0, v1, v2, v3, v4, v5), lists):
        hot = one_hot(idx & (TILE - 1))
        value = jnp.concatenate(split2(ref[...]), axis=0)
        parts = [value * (upper == h).astype(F32).astype(BF16) for h in range(heads)]
        total = total + dot_nt(jnp.concatenate(parts, axis=0), hot)
    for h in range(heads):
        cols = slice(h * TILE, h * TILE + TILE)
        both = total[h * 128 : h * 128 + 64] + total[h * 128 + 64 : h * 128 + 128]
        out_ref[:, cols] = sens_ref[:, cols] + both


def params():
    return pltpu.CompilerParams(vmem_limit_bytes=48 * 1024 * 1024)


def cost(us):
    return pl.CostEstimate(flops=int(us * 5e8), bytes_accessed=int(us * 2e6), transcendentals=0)


def gather_scratch(count, lane_edges):
    return [
        pltpu.VMEM((6, count * 32, 2 * TILE), BF16),
        pltpu.VMEM((12 - lane_edges, count * 16, 2 * TILE), BF16),
        pltpu.VMEM((16 + lane_edges * 16, count * TILE), F32),
    ]


def passed_along(shard, axis, by):
    count = lax.axis_size(axis)
    pairs = [(i, (i + by) % count) for i in range(count)]
    return lax.ppermute(shard, axis, pairs)


def on_device(density, energy, links, send_index, send_live, face_index):
    const = {name: jnp.asarray(value) for name, value in constants().items()}
    blocks = density.shape[1]
    capacity, face_count = send_index.shape[3], face_index.shape[3]
    whole = jax.ShapeDtypeStruct((64, blocks), F32)
    listed = jax.ShapeDtypeStruct((64, capacity), F32)
    faced = jax.ShapeDtypeStruct((64, face_count), F32)
    vmem = pl.BlockSpec(memory_space=pltpu.VMEM)
    smem = pl.BlockSpec(memory_space=pltpu.SMEM)

    loads = pl.pallas_call(
        payload_kernel,
        out_shape=[listed] * 4 + [faced] * 2,
        in_specs=[pl.BlockSpec(memory_space=pl.ANY)] * 4,
        out_specs=[vmem] * 6,
        scratch_shapes=[
            pltpu.SMEM(send_live.shape, jnp.int32),
            pltpu.VMEM(density.shape, F32),
            pltpu.VMEM(send_index.shape, jnp.int32),
            pltpu.VMEM(face_index.shape, jnp.int32),
            pltpu.SemaphoreType.DMA((4,)),
        ],
        compiler_params=pltpu.CompilerParams(vmem_limit_bytes=63 * 1024 * 1024),
        cost_estimate=cost(3),
    )(send_live, density, send_index, face_index)
    received = [passed_along(loads[at], "plane", OFFSETS[g]) for at, g in enumerate(OUTWARD)]
    from_low = passed_along(loads[5], "depth", 1)
    from_high = passed_along(loads[4], "depth", -1)
    part, weight = pl.pallas_call(
        local_kernel,
        out_shape=[whole, whole],
        in_specs=[vmem] * 6,
        out_specs=[vmem] * 2,
        scratch_shapes=gather_scratch(4, LANE_LOCAL),
        compiler_params=params(),
        cost_estimate=cost(8),
    )(density, links, const["fold_fwd"], const["join_fwd"], const["own"], const["sums"])
    part = pl.pallas_call(
        early_kernel,
        out_shape=whole,
        in_specs=[vmem] * 8,
        out_specs=vmem,
        scratch_shapes=gather_scratch(6, LANE_EARLY),
        compiler_params=params(),
        cost_estimate=cost(4),
    )(received[0], received[1], from_low, from_high, links, part, const["fold_fwd"], const["join_fwd"])
    conductivity, scaled, *groups_back = pl.pallas_call(
        remote_kernel,
        out_shape=[whole, whole] + [listed] * 4 + [faced] * 2,
        in_specs=[pl.BlockSpec(memory_space=pl.ANY)] * 2 + [vmem] * 10,
        out_specs=[vmem] * 8,
        scratch_shapes=gather_scratch(4, LANE_REMOTE),
        compiler_params=params(),
        cost_estimate=cost(20),
    )(
        *received, links, part, weight, energy,
        const["fold_fwd"], const["join_fwd"], const["fold_bwd"], const["join_bwd"],
    )
    returned = [passed_along(groups_back[at], "plane", -OFFSETS[g]) for at, g in enumerate(BACKWARD)]
    to_one = passed_along(groups_back[4], "depth", -1)
    to_zero = passed_along(groups_back[5], "depth", 1)
    sens = pl.pallas_call(
        own_kernel,
        out_shape=whole,
        in_specs=[vmem] * 5,
        out_specs=vmem,
        compiler_params=params(),
        cost_estimate=cost(8),
    )(scaled, links, const["fold_bwd"], const["join_bwd"], const["own_t"])
    sens = pl.pallas_call(
        final_kernel,
        out_shape=whole,
        in_specs=[smem] + [vmem] * 9,
        out_specs=vmem,
        compiler_params=params(),
        cost_estimate=cost(3),
    )(send_live, sens, send_index, face_index, *returned, to_zero, to_one)
    return (conductivity, sens)


def solution(mesh):
    in_specs = (
        P(None, ("plane", "depth")),
        P(None, ("plane", "depth")),
        P(None, ("plane", "depth")),
        P("plane", "depth", None, None),
        P("plane", "depth", None),
        P("plane", "depth", None, None),
    )
    out_specs = (P(None, ("plane", "depth")), P(None, ("plane", "depth")))
    return jax.shard_map(
        on_device, mesh=mesh, in_specs=in_specs, out_specs=out_specs, check_vma=False
    )
```

```python
import jax
import jax.numpy as jnp
import numpy as np
from jax import lax
from jax.experimental import pallas as pl
from jax.experimental.pallas import tpu as pltpu
from jax.sharding import PartitionSpec as P

REACH = 2
TILE = 256
OFFSETS = [offset for offset in range(-REACH, REACH + 1) if offset != 0]
OUTWARD = (2, 3, 1, 0)
BACKWARD = (0, 1, 2, 3)
LANE_LOCAL = 6
LANE_EARLY = 7
LANE_REMOTE = 8
radius = 3.0
floor_value = 0.001
penalty = 3.0

F32 = jnp.float32
BF16 = jnp.bfloat16

ORDERS = ((0, 1, 2), (2, 0, 1), (1, 2, 0))


def cone_table():
    voxels = np.arange(64)
    places = np.stack([voxels // 16, voxels // 4 % 4, voxels % 4], axis=-1)
    slots = np.arange(27)
    moved = np.stack([slots // 9 - 1, slots // 3 % 3 - 1, slots % 3 - 1], axis=-1) * 4
    apart = places[None, :, None, :] - places[None, None, :, :] - moved[:, None, None, :]
    squares = np.sum(apart * apart, axis=-1).astype(np.float32)
    return np.maximum(np.float32(0.0), np.float32(radius) - np.sqrt(squares))


def order_voxels(order):
    rows = np.arange(64)
    coords = np.zeros((3, 64), np.int64)
    coords[order[0]], coords[order[1]], coords[order[2]] = rows // 16, rows // 4 % 4, rows % 4
    return coords[0] * 16 + coords[1] * 4 + coords[2]


def slot_of(offset):
    return (offset[0] + 1) * 9 + (offset[1] + 1) * 3 + offset[2] + 1


def layout():
    faces, edges, corners = [], [], []
    for at, order in enumerate(ORDERS):
        for sign in (-1, 1):
            offset = [0, 0, 0]
            offset[order[0]] = sign
            faces.append((slot_of(offset), at, sign))
    for at, order in enumerate(ORDERS):
        for one in (-1, 1):
            for two in (-1, 1):
                offset = [0, 0, 0]
                offset[order[0]], offset[order[1]] = one, two
                edges.append((slot_of(offset), at, one, two))
    for a in (-1, 1):
        for b in (-1, 1):
            for c in (-1, 1):
                corners.append(slot_of((a, b, c)))
    return faces, edges, corners


FACES, EDGES, CORNERS = layout()
SLOTS = [f[0] for f in FACES] + [e[0] for e in EDGES] + CORNERS


def face_start(sign, forward):
    return 32 if (sign > 0) == forward else 0


def edge_starts(one, two, forward):
    first = 2 if (one > 0) == forward else 0
    second = 2 if (two > 0) == forward else 0
    return [(first + i) * 16 + second * 4 for i in range(2)]


def slot_rows(forward):
    voxels = [order_voxels(order) for order in ORDERS]
    out = []
    for slot, at, sign in FACES:
        start = face_start(sign, forward)
        out.append((slot, voxels[at][start : start + 32]))
    for slot, at, one, two in EDGES:
        rows = np.concatenate([voxels[at][s : s + 8] for s in edge_starts(one, two, forward)])
        out.append((slot, rows))
    return out


def pieces_np(table):
    high = table.astype(jnp.bfloat16)
    low = (table - high.astype(np.float32)).astype(jnp.bfloat16)
    return high, low


def three(table):
    high, low = pieces_np(table)
    return np.concatenate([high, low, high], axis=1)


def corner_rows(table, forward):
    out = []
    for slot in CORNERS:
        part = table[slot] if forward else table[slot].T
        counts = (part > 0).sum(axis=1)
        main = int(np.argmax(counts))
        rest = [int(v) for v in np.nonzero(counts)[0] if v != main]
        out.append((part, main, rest))
    return out


def constants():
    table = cone_table()
    fold_fwd = [table[slot][rows] for slot, rows in slot_rows(True)]
    fold_bwd = [table[slot].T[rows] for slot, rows in slot_rows(False)]
    cor_fwd, cor_bwd = corner_rows(table, True), corner_rows(table, False)
    fold_fwd += [np.stack([part[main] for part, main, rest in cor_fwd])]
    fold_fwd += [np.stack([part[rest[0]] for part, main, rest in cor_fwd])]
    for part, main, rest in cor_bwd:
        fold_bwd += [np.tile(np.stack([part[main], part[rest[0]]]), (8, 1))]
    spots = []
    for at in (1, 2):
        spot = np.zeros((64, 64), np.float32)
        spot[order_voxels(ORDERS[at]), np.arange(64)] = 1
        spots.append(spot)
    cf = np.zeros((64, 16), np.float32)
    for m, (part, main, rest) in enumerate(cor_fwd):
        cf[main, m] = 1
        cf[rest, 8 + m] = 1
    join_fwd = np.concatenate(spots + [cf], axis=1)
    join_fwd = np.concatenate([join_fwd, join_fwd], axis=1).astype(jnp.bfloat16)
    joins = []
    for parity in range(2):
        cb = np.zeros((64, 64), np.float32)
        for m, (part, main, rest) in enumerate(cor_bwd):
            for piece in range(2):
                cb[main, m * 8 + parity * 4 + piece * 2] = 1
                cb[rest, m * 8 + parity * 4 + piece * 2 + 1] = 1
        join = np.concatenate(spots + [cb], axis=1)
        joins.append(np.concatenate([join, join], axis=1))
    sums = table.sum(axis=2).T
    high, low = pieces_np(sums)
    return dict(
        fold_fwd=three(np.concatenate(fold_fwd)),
        fold_bwd=three(np.concatenate(fold_bwd)),
        own=three(table[13]),
        own_t=three(table[13].T),
        join_fwd=join_fwd,
        join_bwd=np.concatenate(joins).astype(jnp.bfloat16),
        sums=np.concatenate([high, low], axis=1),
    )


def split2(value):
    high = value.astype(BF16)
    return high, (value - high.astype(F32)).astype(BF16)


def pieces(value):
    high, low = split2(value)
    return jnp.concatenate([high, high, low], axis=0)


def dot(a, b):
    return jnp.dot(a, b, preferred_element_type=F32)


def dot_nt(a, b):
    return lax.dot_general(a, b, (((1,), (1,)), ((), ())), preferred_element_type=F32)


def one_hot(low):
    shape = (TILE, low.shape[1])
    low = low.astype(jnp.int16)
    hit = lax.broadcasted_iota(jnp.int16, shape, 0) == jnp.broadcast_to(low, shape)
    return jnp.where(hit, jnp.array(1, BF16), jnp.array(0, BF16))


def gather_filtered(chunks, ids, lane_edges, links_ref, fold_ref, join_ref, tf, te, yc):
    count = len(chunks)
    faces, edges = len(FACES), len(EDGES)
    blocks = links_ref.shape[1]
    cut = 192 + (edges - lane_edges) * 16
    for h, chunk in enumerate(chunks):
        y = dot(fold_ref[...], pieces(chunk))
        high, low = split2(y[:cut])
        for f in range(faces):
            tf[f, h * 32 : h * 32 + 32, 0:TILE] = high[f * 32 : f * 32 + 32]
            tf[f, h * 32 : h * 32 + 32, TILE : 2 * TILE] = low[f * 32 : f * 32 + 32]
        for e in range(edges - lane_edges):
            at = 192 + e * 16
            te[e, h * 16 : h * 16 + 16, 0:TILE] = high[at : at + 16]
            te[e, h * 16 : h * 16 + 16, TILE : 2 * TILE] = low[at : at + 16]
        yc[:, h * TILE : h * TILE + TILE] = y[cut:400]

    def by_matmul(slot, table, rows):
        out = []
        for nb in range(blocks // TILE):
            idx = links_ref[slot : slot + 1, nb * TILE : nb * TILE + TILE]
            hot = one_hot(idx & (TILE - 1))
            upper = jnp.broadcast_to(idx >> 8, (rows, TILE))
            got = dot(table[:, 0:TILE], hot) + dot(table[:, TILE : 2 * TILE], hot)
            acc = jnp.zeros((rows, TILE), F32)
            for h in range(count):
                acc = jnp.where(upper == ids[h], got[h * rows : h * rows + rows], acc)
            out.append(acc)
        return jnp.concatenate(out, axis=1)

    def by_lanes(index_of, at, groups):
        out = [[] for _ in range(groups)]
        for bg in range(blocks // 128):
            idx = index_of(slice(bg * 128, bg * 128 + 128))
            low, upper = idx & 127, idx >> 7
            acc = [jnp.zeros((8, 128), F32) for _ in range(groups)]
            for h in range(2 * count):
                hit = upper == 2 * ids[h // 2] + h % 2
                for c in range(groups):
                    rows = slice(at + c * 8, at + c * 8 + 8)
                    got = jnp.take_along_axis(yc[rows, h * 128 : h * 128 + 128], low, axis=1)
                    acc[c] = jnp.where(hit, got, acc[c])
            for c in range(groups):
                out[c].append(acc[c])
        return jnp.concatenate([jnp.concatenate(c, axis=1) for c in out], axis=0)

    def edge_lanes(e):
        slot = EDGES[e][0]
        at = (e - edges + lane_edges) * 16
        return by_lanes(
            lambda cols: jnp.broadcast_to(links_ref[slot : slot + 1, cols], (8, 128)), at, 2
        )

    def corner_index(cols):
        return jnp.concatenate([links_ref[slot : slot + 1, cols] for slot in CORNERS], axis=0)

    lanes = [(edge_lanes, e) for e in range(edges - lane_edges, edges)]
    lanes.append((lambda _: by_lanes(corner_index, lane_edges * 16, 2), "corner"))
    matmuls = [(FACES[f][0], tf.at[f], 32, f) for f in range(faces)]
    matmuls += [(EDGES[e][0], te.at[e], 16, faces + e) for e in range(edges - lane_edges)]
    found = {}
    done = 0
    for i, (slot, table, rows, name) in enumerate(matmuls):
        found[name] = by_matmul(slot, table, rows)
        while done < len(lanes) and done * len(matmuls) <= i * len(lanes):
            fn, e = lanes[done]
            found[e if e == "corner" else faces + e] = fn(e)
            done += 1
    for fn, e in lanes[done:]:
        found[e if e == "corner" else faces + e] = fn(e)
    totals = order_totals(lambda f: found[f], lambda e: found[faces + e], True)
    high, low = split2(jnp.concatenate([totals[1], totals[2], found["corner"]], axis=0))
    return totals[0] + dot(join_ref[...], jnp.concatenate([high, low], axis=0))


def order_totals(face, edge, forward):
    totals = []
    for at in range(3):
        runs = [None] * 8
        for f, (_, order, sign) in enumerate(FACES):
            if order == at:
                value, start = face(f), face_start(sign, forward)
                for i in range(4):
                    runs[start // 8 + i] = value[i * 8 : i * 8 + 8]
        for e, (_, order, one, two) in enumerate(EDGES):
            if order == at:
                value = edge(e)
                for i, start in enumerate(edge_starts(one, two, forward)):
                    runs[start // 8] = runs[start // 8] + value[i * 8 : i * 8 + 8]
        totals.append(jnp.concatenate(runs, axis=0))
    return totals


def scatter_back(scaled, ids, kind, links_ref, fold_ref, join_ref):
    count = len(ids)
    blocks = links_ref.shape[1]
    spread = dot(fold_ref[...], pieces(scaled))
    lows = jnp.transpose((links_ref[...] & (TILE - 1)).astype(F32))
    lane = lax.broadcasted_iota(jnp.int32, (blocks, TILE), 1).astype(F32).astype(kind)

    def hot_rows(slot):
        low = jnp.broadcast_to(lows[:, slot : slot + 1], (blocks, TILE)).astype(kind)
        return jnp.where(lane == low, jnp.array(1, kind), jnp.array(0, kind)).astype(BF16)


    quarter = lax.broadcasted_iota(jnp.int32, (16, blocks), 0) // 4
    quarters = []
    for q in range((count + 3) // 4):
        rows_for = jnp.full((16, blocks), -1, jnp.int32)
        for i, h in enumerate(ids[4 * q : 4 * q + 4]):
            rows_for = jnp.where(quarter == i, h, rows_for)
        quarters.append(rows_for)

    def one_slot(slot, value, rows):
        idx = links_ref[slot : slot + 1, :]
        hot = hot_rows(slot)
        upper = idx >> 8
        parts = [value * (upper == h).astype(F32).astype(BF16) for h in ids]
        got = dot(jnp.concatenate(parts, axis=0), hot)
        return [
            got[h * 2 * rows : h * 2 * rows + rows] + got[h * 2 * rows + rows : h * 2 * rows + 2 * rows]
            for h in range(count)
        ]

    def one_corner(m):
        idx = links_ref[CORNERS[m] : CORNERS[m] + 1, :]
        hot = hot_rows(CORNERS[m])
        upper = jnp.broadcast_to(idx >> 8, (16, blocks))
        is_high = lax.broadcasted_iota(jnp.int32, (16, blocks), 0) % 4 < 2
        part = spread[384 + m * 16 : 384 + m * 16 + 16]
        top = part.astype(BF16).astype(F32)
        value = jnp.where(is_high, top, part - top).astype(BF16)
        parts = [
            value * (upper == quarters[q]).astype(F32).astype(BF16) for q in range(len(quarters))
        ]
        return dot(jnp.concatenate(parts, axis=0), hot)

    def both(at, rows):
        return jnp.concatenate(split2(spread[at : at + rows]), axis=0)

    faces = [one_slot(face[0], both(f * 32, 32), 32) for f, face in enumerate(FACES)]
    edges = [one_slot(edge[0], both(192 + e * 16, 16), 16) for e, edge in enumerate(EDGES)]
    corners = [one_corner(m) for m in range(len(CORNERS))]
    out = []
    for h in range(count):
        totals = order_totals(lambda f: faces[f][h], lambda e: edges[e][h], False)
        tops = [corner[h // 2 * 8 : h // 2 * 8 + 8] for corner in corners]
        high, low = split2(jnp.concatenate([totals[1], totals[2]] + tops, axis=0))
        join = join_ref[h % 2 * 64 : h % 2 * 64 + 64, :]
        out.append(totals[0] + dot(join, jnp.concatenate([high, low], axis=0)))
    return out


def chunk_ids(order, heads):
    out = []
    for g in order:
        out += [heads + 2 * g, heads + 2 * g + 1]
    return out + [heads + 8, heads + 9]


def list_uppers(order, live_ref, index_ref, face_ref):
    place, places = lax.axis_index("plane"), lax.axis_size("plane")
    level, levels = lax.axis_index("depth"), lax.axis_size("depth")
    out = []
    for g in order:
        offset = OFFSETS[g]
        idx = index_ref[0, 0, g : g + 1, :]
        target = place + offset
        live = jnp.where((target >= 0) & (target < places), live_ref[0, 0, g], 0)
        at = lax.broadcasted_iota(jnp.int32, idx.shape, 1)
        out.append((idx, jnp.where(at < live, idx >> 8, -1)))
    for side, by in enumerate((-1, 1)):
        idx = face_ref[0, 0, side : side + 1, :]
        target = level + by
        live = jnp.where((target >= 0) & (target < levels), idx.shape[1], 0)
        at = lax.broadcasted_iota(jnp.int32, idx.shape, 1)
        out.append((idx, jnp.where(at < live, idx >> 8, -1)))
    return out


def payload_kernel(live_hbm, density_hbm, index_hbm, face_hbm, *refs):
    outs = refs[:6]
    live_ref, density_ref, index_ref, face_ref, sems = refs[6:]
    copies = [
        pltpu.make_async_copy(source, target, sems.at[at])
        for at, (source, target) in enumerate(
            [(density_hbm, density_ref), (live_hbm, live_ref), (index_hbm, index_ref), (face_hbm, face_ref)]
        )
    ]
    for copy in copies:
        copy.start()
    for copy in copies:
        copy.wait()
    density = density_ref[...]
    high, low = split2(density)
    heads = density.shape[1] // TILE
    table = jnp.concatenate(
        [
            jnp.concatenate([p[:, h * TILE : h * TILE + TILE] for h in range(heads)], axis=0)
            for p in (high, low)
        ],
        axis=1,
    )
    for ref, (idx, upper) in zip(outs, list_uppers(OUTWARD, live_ref, index_ref, face_ref)):
        hot = one_hot(idx & (TILE - 1))
        got = dot(table[:, 0:TILE], hot) + dot(table[:, TILE : 2 * TILE], hot)
        upper = jnp.broadcast_to(upper, (64, idx.shape[1]))
        acc = jnp.zeros((64, idx.shape[1]), F32)
        for h in range(heads):
            acc = jnp.where(upper == h, got[h * 64 : h * 64 + 64], acc)
        ref[...] = acc


def local_kernel(
    density_ref, links_ref, fold_ref, join_ref, own_ref, sums_ref, part_ref, weight_ref, *scratch
):
    density = density_ref[...]
    heads = density.shape[1] // TILE
    chunks = [density[:, h * TILE : h * TILE + TILE] for h in range(heads)]
    part = gather_filtered(chunks, list(range(heads)), LANE_LOCAL, links_ref, fold_ref, join_ref, *scratch)
    part_ref[...] = part + dot(own_ref[...], pieces(density))
    valid = (links_ref[...] != 14 * TILE).astype(F32).astype(BF16)
    weight_ref[...] = dot(sums_ref[...], jnp.concatenate([valid, valid], axis=0))


def tile_chunks(refs):
    return [ref[:, at : at + TILE] for ref in refs for at in range(0, ref.shape[1], TILE)]


def early_kernel(r0, r1, low_ref, high_ref, links_ref, part_ref, fold_ref, join_ref, out_ref, *scratch):
    ids = chunk_ids(OUTWARD, part_ref.shape[1] // TILE)
    chunks = tile_chunks((r0, r1, low_ref, high_ref))
    total = gather_filtered(chunks, ids[:4] + ids[8:], LANE_EARLY, links_ref, fold_ref, join_ref, *scratch)
    out_ref[...] = part_ref[...] + total


def remote_kernel(
    r0, r1, r2, r3, links_ref, part_ref, weight_ref, energy_ref,
    fold_ref, join_ref, fold_b_ref, join_b_ref,
    cond_ref, scaled_ref, b0, b1, b2, b3, lb, ub, *scratch,
):
    heads = part_ref.shape[1] // TILE
    chunks = tile_chunks((r2, r3))
    total = gather_filtered(chunks, chunk_ids(OUTWARD, heads)[4:8], LANE_REMOTE, links_ref, fold_ref, join_ref, *scratch)
    weight = weight_ref[...]
    filtered = (part_ref[...] + total) / weight
    square = filtered * filtered
    cond_ref[...] = floor_value + square * filtered * (1.0 - floor_value)
    scaled = -penalty * (1.0 - floor_value) * square * energy_ref[...] / weight
    scaled_ref[...] = scaled
    back = scatter_back(scaled, chunk_ids(BACKWARD, heads), F32, links_ref, fold_b_ref, join_b_ref)
    at = 0
    for ref in (b0, b1, b2, b3, lb, ub):
        for start in range(0, ref.shape[1], TILE):
            ref[:, start : start + TILE] = back[at]
            at += 1


def own_kernel(scaled_ref, links_ref, fold_b_ref, join_b_ref, own_ref, sens_ref):
    scaled = scaled_ref[...]
    heads = scaled.shape[1] // TILE
    back = scatter_back(scaled, list(range(heads)), BF16, links_ref, fold_b_ref, join_b_ref)
    sens_ref[...] = jnp.concatenate(back, axis=1) + dot(own_ref[...], pieces(scaled))


def final_kernel(live_ref, sens_ref, index_ref, face_ref, v0, v1, v2, v3, v4, v5, out_ref):
    heads = sens_ref.shape[1] // TILE
    total = jnp.zeros((heads * 128, TILE), F32)
    lists = list_uppers(BACKWARD, live_ref, index_ref, face_ref)
    for ref, (idx, upper) in zip((v0, v1, v2, v3, v4, v5), lists):
        hot = one_hot(idx & (TILE - 1))
        value = jnp.concatenate(split2(ref[...]), axis=0)
        parts = [value * (upper == h).astype(F32).astype(BF16) for h in range(heads)]
        total = total + dot_nt(jnp.concatenate(parts, axis=0), hot)
    for h in range(heads):
        cols = slice(h * TILE, h * TILE + TILE)
        both = total[h * 128 : h * 128 + 64] + total[h * 128 + 64 : h * 128 + 128]
        out_ref[:, cols] = sens_ref[:, cols] + both


def params():
    return pltpu.CompilerParams(vmem_limit_bytes=48 * 1024 * 1024)


def cost(us):
    return pl.CostEstimate(flops=int(us * 5e8), bytes_accessed=int(us * 2e6), transcendentals=0)


def gather_scratch(count, lane_edges):
    return [
        pltpu.VMEM((6, count * 32, 2 * TILE), BF16),
        pltpu.VMEM((12 - lane_edges, count * 16, 2 * TILE), BF16),
        pltpu.VMEM((16 + lane_edges * 16, count * TILE), F32),
    ]


def passed_along(shard, axis, by):
    count = lax.axis_size(axis)
    pairs = [(i, (i + by) % count) for i in range(count)]
    return lax.ppermute(shard, axis, pairs)


def on_device(density, energy, links, send_index, send_live, face_index):
    const = {name: jnp.asarray(value) for name, value in constants().items()}
    blocks = density.shape[1]
    capacity, face_count = send_index.shape[3], face_index.shape[3]
    whole = jax.ShapeDtypeStruct((64, blocks), F32)
    listed = jax.ShapeDtypeStruct((64, capacity), F32)
    faced = jax.ShapeDtypeStruct((64, face_count), F32)
    vmem = pl.BlockSpec(memory_space=pltpu.VMEM)
    smem = pl.BlockSpec(memory_space=pltpu.SMEM)

    loads = pl.pallas_call(
        payload_kernel,
        out_shape=[listed] * 4 + [faced] * 2,
        in_specs=[pl.BlockSpec(memory_space=pl.ANY)] * 4,
        out_specs=[vmem] * 6,
        scratch_shapes=[
            pltpu.SMEM(send_live.shape, jnp.int32),
            pltpu.VMEM(density.shape, F32),
            pltpu.VMEM(send_index.shape, jnp.int32),
            pltpu.VMEM(face_index.shape, jnp.int32),
            pltpu.SemaphoreType.DMA((4,)),
        ],
        compiler_params=pltpu.CompilerParams(vmem_limit_bytes=63 * 1024 * 1024),
        cost_estimate=cost(3),
    )(send_live, density, send_index, face_index)
    received = [passed_along(loads[at], "plane", OFFSETS[g]) for at, g in enumerate(OUTWARD)]
    from_low = passed_along(loads[5], "depth", 1)
    from_high = passed_along(loads[4], "depth", -1)
    part, weight = pl.pallas_call(
        local_kernel,
        out_shape=[whole, whole],
        in_specs=[vmem] * 6,
        out_specs=[vmem] * 2,
        scratch_shapes=gather_scratch(4, LANE_LOCAL),
        compiler_params=params(),
        cost_estimate=cost(8),
    )(density, links, const["fold_fwd"], const["join_fwd"], const["own"], const["sums"])
    part = pl.pallas_call(
        early_kernel,
        out_shape=whole,
        in_specs=[vmem] * 8,
        out_specs=vmem,
        scratch_shapes=gather_scratch(6, LANE_EARLY),
        compiler_params=params(),
        cost_estimate=cost(4),
    )(received[0], received[1], from_low, from_high, links, part, const["fold_fwd"], const["join_fwd"])
    conductivity, scaled, *groups_back = pl.pallas_call(
        remote_kernel,
        out_shape=[whole, whole] + [listed] * 4 + [faced] * 2,
        in_specs=[pl.BlockSpec(memory_space=pl.ANY)] * 2 + [vmem] * 10,
        out_specs=[vmem] * 8,
        scratch_shapes=gather_scratch(4, LANE_REMOTE),
        compiler_params=params(),
        cost_estimate=cost(20),
    )(
        *received, links, part, weight, energy,
        const["fold_fwd"], const["join_fwd"], const["fold_bwd"], const["join_bwd"],
    )
    returned = [passed_along(groups_back[at], "plane", -OFFSETS[g]) for at, g in enumerate(BACKWARD)]
    to_one = passed_along(groups_back[4], "depth", -1)
    to_zero = passed_along(groups_back[5], "depth", 1)
    sens = pl.pallas_call(
        own_kernel,
        out_shape=whole,
        in_specs=[vmem] * 5,
        out_specs=vmem,
        compiler_params=params(),
        cost_estimate=cost(8),
    )(scaled, links, const["fold_bwd"], const["join_bwd"], const["own_t"])
    sens = pl.pallas_call(
        final_kernel,
        out_shape=whole,
        in_specs=[smem] + [vmem] * 9,
        out_specs=vmem,
        compiler_params=params(),
        cost_estimate=cost(3),
    )(send_live, sens, send_index, face_index, *returned, to_zero, to_one)
    return (conductivity, sens)


def solution(mesh):
    in_specs = (
        P(None, ("plane", "depth")),
        P(None, ("plane", "depth")),
        P(None, ("plane", "depth")),
        P("plane", "depth", None, None),
        P("plane", "depth", None),
        P("plane", "depth", None, None),
    )
    out_specs = (P(None, ("plane", "depth")), P(None, ("plane", "depth")))
    return jax.shard_map(
        on_device, mesh=mesh, in_specs=in_specs, out_specs=out_specs, check_vma=False
    )
```
